32 devices in a mesh: gx: 4 (over y, x), gy: 8 (over z, core).
Axes of the slice: x: 2, y: 2, z: 4, core: 2. Of those that a mesh axis runs over, the one named last changes fastest.
Arguments:
- vorticity: float32 [3, 128, 256, 256], P(None, 'gx', 'gy'), may hold values from -6 to 6
- velocity_old: float32 [3, 128, 256, 256], P(None, 'gx', 'gy'), may hold values from -6 to 6
- green_hat: float32 [512, 512], P(None, 'gy'), may hold values from 0.45 to 10.5, as said below
Outputs:
- vorticity_new: float32 [3, 128, 256, 256], P(None, 'gx', 'gy')
- velocity: float32 [3, 128, 256, 256], P(None, 'gx', 'gy')
The draws below stay inside these ranges and needn't reach their ends.
Inputs may be any that keep to these rules, and one draw needn't show every extreme that they name: green_hat[(512 - m) mod (512), (512 - k) mod (512)] equals green_hat[m, k].
All inputs are finite; a program needn't handle non-finite values.
Results may differ from the reference program's by a relative error of at most 0.000059.
Values sent between devices are 32-bit elements; how exact they have to be, the bound alone decides.
No kernel may reach another device: no remote copies, remote signals or barrier semaphores. Data moves between devices by JAX's collectives and lax.ppermute only.
A program may use at most 192 MiB of HBM per device.

```python
import math
import jax
import jax.numpy as jnp
from jax import lax

NY = 256
NZ = 256
NX = 128


def draw_green_hat(key, part):
    padded_rows = 2 * NY
    padded_depth = 2 * NZ
    base = jnp.exp(jax.random.uniform(key, (padded_rows, padded_depth), jnp.float32, math.log(0.5), math.log(2.0)))
    mirror = jnp.roll(jnp.flip(base, (0, 1)), 1, (0, 1))
    row_index = jnp.arange(padded_rows, dtype=jnp.int32)
    depth_index = jnp.arange(padded_depth, dtype=jnp.int32)
    fold_rows = jnp.minimum(row_index, padded_rows - row_index).astype(jnp.float32)
    fold_depth = jnp.minimum(depth_index, padded_depth - depth_index).astype(jnp.float32)
    radius = fold_rows[:, None] * fold_rows[:, None] + fold_depth[None, :] * fold_depth[None, :]
    smooth = 1.0 + 4.0 / (1.0 + radius / 64.0)
    return (0.5 * (base + mirror) * smooth).astype(jnp.float32)


def levels(own_key, extent, pieces, least, high):
    level, own = 1.0, jax.random.fold_in(own_key, 6)
    for dim, parts in pieces:
        steps = jnp.exp(jax.random.uniform(jax.random.fold_in(own, dim), (parts,), jnp.float32, least / len(pieces), high / len(pieces)))
        level = level * jnp.repeat(steps, extent[dim] // parts).reshape([-1 if axis == dim else 1 for axis in range(len(extent))])
    return level


def gaussian(rng, extent, deviation, bound, shards=(), kind=jnp.bfloat16):
    drawn = jax.random.normal(rng, extent, jnp.float32) * deviation
    if len(shards) > 0:
        drawn = levels(rng, extent, shards, -0.22, 0.18) * drawn
    return jnp.clip(drawn, min=-bound, max=bound).astype(kind)


def setup_inputs(seed: int = 0) -> dict:
    key_of = jax.random.split(jax.random.key(seed), 4)
    return {
        "vorticity": gaussian(key_of[0], (3, NX, NY, NZ), 1.0, 6.0, ((1, 4), (2, 8)), jnp.float32),
        "velocity_old": gaussian(key_of[1], (3, NX, NY, NZ), 1.0, 6.0, ((1, 4), (2, 8)), jnp.float32),
        "green_hat": draw_green_hat(jax.random.fold_in(key_of[3], 71), 0),
    }


time_step = 0.2
viscosity = 0.1


def neighbours(field):
    framed = jnp.pad(field, ((0, 0), (1, 1), (1, 1), (1, 1)))
    return (framed[:, 2:, 1:-1, 1:-1], framed[:, :-2, 1:-1, 1:-1],
            framed[:, 1:-1, 2:, 1:-1], framed[:, 1:-1, :-2, 1:-1],
            framed[:, 1:-1, 1:-1, 2:], framed[:, 1:-1, 1:-1, :-2])


def derivatives(field):
    near = neighbours(field)
    return (0.5 * (near[0] - near[1]), 0.5 * (near[2] - near[3]), 0.5 * (near[4] - near[5]))


def reference(vorticity, velocity_old, green_hat):
    grad_x, grad_y, grad_z = derivatives(velocity_old)
    stretch = vorticity[0:1] * grad_x + vorticity[1:2] * grad_y + vorticity[2:3] * grad_z
    near = neighbours(vorticity)
    laplace = near[0] + near[1] + near[2] + near[3] + near[4] + near[5] - 6.0 * vorticity
    vorticity_new = vorticity + time_step * (stretch + viscosity * laplace)
    stacked_planes = jnp.moveaxis(vorticity_new, 1, 0)

    def solve_plane(plane):
        padded = jnp.pad(plane, ((0, 0), (0, NY), (0, NZ)))
        spectrum = jnp.fft.fft2(padded, axes=(1, 2))
        field = jnp.fft.ifft2(spectrum * green_hat, axes=(1, 2))
        return jnp.real(field)[:, :NY, :NZ]

    psi = jnp.moveaxis(lax.map(solve_plane, stacked_planes), 0, 1)
    psi_x, psi_y, psi_z = derivatives(psi)
    velocity = jnp.stack([psi_y[2] - psi_z[1], psi_z[0] - psi_x[2], psi_x[1] - psi_y[0]])
    return vorticity_new, velocity
```

```python
import functools
import math

import jax
import jax.numpy as jnp
import ml_dtypes
import numpy as np
from jax import lax
from jax.experimental import pallas as pl
from jax.experimental.pallas import tpu as pltpu
from jax.sharding import PartitionSpec as P

time_step = 0.2
viscosity = 0.1
radix = 4
VMEM = pltpu.VMEM
SMEM = pltpu.SMEM
limit = 56 * 1024 * 1024


def params():
    return pltpu.CompilerParams(vmem_limit_bytes=limit)


def in_vmem(count):
    return [pl.BlockSpec(memory_space=VMEM)] * count


def halves_np(matrix, axis):


    value = np.asarray(matrix, np.float32)
    high = value.astype(ml_dtypes.bfloat16)
    low = (value - high.astype(np.float32)).astype(ml_dtypes.bfloat16)
    return np.concatenate([high, high, low], axis=axis)


def parts(value, axis):
    high = value.astype(jnp.bfloat16)
    low = (value - high.astype(jnp.float32)).astype(jnp.bfloat16)
    return jnp.concatenate([high, low, high], axis=axis)


@functools.lru_cache(maxsize=None)
def constants(rows, depth):
    long_z, long_y = 2 * depth, 2 * rows
    half = long_y // radix
    k = np.arange(depth)[:, None]
    z = np.arange(depth)[None, :]
    turn = 2.0 * np.pi * (((2 * k + 1) * z) % (2 * long_z)) / (2 * long_z)
    forward_z = halves_np(np.concatenate([np.cos(turn), -np.sin(turn)], axis=0), 1)
    inverse_z = np.concatenate([np.cos(turn), -np.sin(turn)], axis=0) * (2.0 / long_z)
    inverse_z = halves_np(inverse_z.T, 1)
    b = np.arange(half)[:, None]
    p = np.arange(half)[None, :]
    ahead, back = [], []
    for q in range(radix):
        angle = 2.0 * np.pi * ((b * (radix * p + q)) % long_y) / long_y
        c, s = np.cos(angle), np.sin(angle)
        ahead.append(halves_np(np.block([[c, -s], [s, c]]), 0))
        c, s = c.T / long_y, s.T / long_y
        back.append(halves_np(np.block([[c, s], [-s, c]]), 0))
    shift = np.arange(depth)[:, None] + 0.5 - np.arange(long_z)[None, :]
    d = np.arange(1, depth)
    table = 1.0 + 2.0 * np.cos(2.0 * np.pi * np.arange(-2 * long_z, 2 * long_z)[:, None] * d[None, :] / (2 * long_z)).sum(1)
    index = np.rint(2 * shift).astype(np.int64) + 2 * long_z
    dirichlet = (table[index] / long_z).astype(np.float32)
    return forward_z, inverse_z, np.stack(ahead), np.stack(back), dirichlet


def plane_of(owner, chunk, local, chunks, width):
    if chunks == 1:
        return owner * width + local
    return owner * width * chunks + lax.bitwise_xor(owner & 1, chunk) * width + local


def advance_kernel(chunk, chunks, whole, me_ref, vort, vel, ylo, yhi, xlo, xhi, *rest):
    _, planes, band, depth = vort.shape
    if whole:
        new, sends = rest[0], rest[1:]
    else:
        sends, new = rest[:-1], rest[-1]
    groups = len(sends)
    width = sends[0].shape[1]
    me = me_ref[0]
    row = lax.broadcasted_iota(jnp.int32, (band, depth), 0)
    column = lax.broadcasted_iota(jnp.int32, (band, depth), 1)
    first_row, last_row = row == 0, row == band - 1
    first_column, last_column = column == 0, column == depth - 1

    def neighbours(source, comp, slot, x):
        here = source[comp, x]
        before = jnp.where(x > 0, source[comp, jnp.maximum(x - 1, 0)], xlo[slot])
        after = jnp.where(x < planes - 1, source[comp, jnp.minimum(x + 1, planes - 1)], xhi[slot])
        down = jnp.where(first_row, ylo[slot, pl.ds(x, 1), :], pltpu.roll(here, 1, 0))
        up = jnp.where(last_row, yhi[slot, pl.ds(x, 1), :], pltpu.roll(here, band - 1, 0))
        left = jnp.where(first_column, 0.0, pltpu.roll(here, 1, 1))
        right = jnp.where(last_column, 0.0, pltpu.roll(here, depth - 1, 1))
        return here, after, before, up, down, right, left

    def step(t, carry):
        if whole:
            x = t
        else:
            x = plane_of(t // width, chunk, t % width, chunks, width)
        w = [vort[c, x] for c in range(3)]
        for c in range(3):
            _, xp, xm, yp, ym, zp, zm = neighbours(vel, c, 3 + c, x)
            stretch = 0.5 * (w[0] * (xp - xm) + w[1] * (yp - ym) + w[2] * (zp - zm))
            here, xp, xm, yp, ym, zp, zm = neighbours(vort, c, c, x)
            laplace = xp + xm + yp + ym + zp + zm - 6.0 * here
            new[c, x] = here + time_step * (stretch + viscosity * laplace)
        return carry

    lax.fori_loop(0, planes if whole else groups * width, step, 0)
    for d in range(groups):
        owner = lax.bitwise_xor(me, d)
        for s in range(width):
            x = plane_of(owner, chunk, s, chunks, width)
            for c in range(3):
                sends[d][c, s] = new[c, x]


def advance(chunk, chunks, whole, me, groups, vort, vel, halos):
    _, planes, band, depth = vort.shape
    width = planes // groups // chunks
    block = jax.ShapeDtypeStruct((3, width, band, depth), jnp.float32)
    shapes = [block] * groups
    scratch = []
    if whole:
        shapes = [jax.ShapeDtypeStruct(vort.shape, jnp.float32)] + shapes
    else:
        scratch = [pltpu.VMEM(vort.shape, jnp.float32)]
    return pl.pallas_call(
        functools.partial(advance_kernel, chunk, chunks, whole),
        out_shape=shapes,
        in_specs=[pl.BlockSpec(memory_space=SMEM)] + in_vmem(6),
        out_specs=in_vmem(len(shapes)),
        scratch_shapes=scratch,
        compiler_params=params(),
        name=f"advance_{chunk}",
    )(me, vort, vel, *halos)


def solve_kernel(groups, me_ref, fz, bz, ey, by, green, *refs):
    sources, targets = refs[:groups], refs[groups : 2 * groups]
    plane, psi = refs[2 * groups :]
    _, width, band, depth = sources[0].shape
    rows = band * groups
    half = rows // 2
    me = me_ref[0]
    pad = 8
    halo_base = 3 * width * band
    zeros = jnp.zeros((pad, depth), jnp.float32)
    psi[pl.ds(0, pad), :] = zeros
    psi[pl.ds(pad + rows, pad), :] = zeros

    def step(t, carry):
        c, s = t // width, t % width
        for d in range(groups):
            start = pl.multiple_of(lax.bitwise_xor(me, d) * band, band)
            plane[pl.ds(start, band), :] = sources[d][c, s]
        spectrum = lax.dot_general(
            fz[...], parts(plane[...], 1), (((1,), (1,)), ((), ())), preferred_element_type=jnp.float32
        )
        low_r, high_r = spectrum[:depth, :half], spectrum[:depth, half:]
        low_i, high_i = spectrum[depth:, :half], spectrum[depth:, half:]
        turned = [
            (low_r + high_r, low_i + high_i),
            (low_r + high_i, low_i - high_r),
            (low_r - high_r, low_i - high_i),
            (low_r - high_i, low_i + high_r),
        ]
        total = None
        for q in range(radix):
            data = parts(jnp.concatenate(turned[q], axis=1), 1)
            freq = jnp.dot(data, ey[q], preferred_element_type=jnp.float32)
            gain = green[:, q * half : (q + 1) * half]
            freq = jnp.concatenate([freq[:, :half] * gain, freq[:, half:] * gain], axis=1)
            out = jnp.dot(parts(freq, 1), by[q], preferred_element_type=jnp.float32)
            re, im = out[:, :half], out[:, half:]
            second = [(re, im), (-im, re), (-re, -im), (im, -re)][q]
            mine = (re, im) + second
            total = mine if total is None else tuple(a + b for a, b in zip(total, mine))
        stacked = jnp.concatenate(
            [jnp.concatenate([total[0], total[2]], axis=1), jnp.concatenate([total[1], total[3]], axis=1)], axis=0
        )
        result = jnp.dot(bz[...], parts(stacked, 0), preferred_element_type=jnp.float32)
        psi[pl.ds(pad, rows), :] = result.T
        offset = pl.multiple_of((c * width + s) * band, band)
        edge = halo_base + ((c // 2) * width + s) * 2
        for d in range(groups):
            start = lax.bitwise_xor(me, d) * band
            targets[d][pl.ds(offset, band), :] = psi[pl.ds(pl.multiple_of(start + pad, pad), band), :]

            @pl.when(c != 1)
            def _():
                targets[d][pl.ds(edge, 1), :] = psi[pl.ds(start + pad - 1, 1), :]
                targets[d][pl.ds(edge + 1, 1), :] = psi[pl.ds(start + pad + band, 1), :]

        return carry

    lax.fori_loop(0, 3 * width, step, 0)


def solve(me, green, tables, blocks):
    groups = len(blocks)
    _, width, band, depth = blocks[0].shape
    rows = band * groups
    lines = 3 * width * band + 4 * width
    shape = jax.ShapeDtypeStruct((lines, depth), jnp.float32)
    return pl.pallas_call(
        functools.partial(solve_kernel, groups),
        out_shape=[shape] * groups,
        in_specs=[pl.BlockSpec(memory_space=SMEM)] + in_vmem(5 + groups),
        out_specs=in_vmem(groups),
        scratch_shapes=[pltpu.VMEM((rows, depth), jnp.float32), pltpu.VMEM((rows + 16, depth), jnp.float32)],
        compiler_params=params(),
        name="solve",
    )(me, *tables, green, *blocks)


def curl_kernel(groups, chunks, band, width, me_ref, xlo, xhi, *refs):
    blocks = refs[: groups * chunks]
    velocity, psi, edge = refs[groups * chunks :]
    planes, depth = velocity.shape[1], velocity.shape[3]
    me = me_ref[0]
    halo_base = 3 * width * band
    for k in range(chunks):
        for d in range(groups):
            owner = lax.bitwise_xor(me, d)
            block = blocks[k * groups + d]
            for s in range(width):
                x = plane_of(owner, k, s, chunks, width)
                for c in range(3):
                    psi[c, x + 1] = block[pl.ds((c * width + s) * band, band), :]
                for h in range(2):
                    edge[h, x] = block[pl.ds(halo_base + (h * width + s) * 2, 2), :]
    for h in range(2):
        psi[h + 1, 0] = xlo[h]
        psi[h + 1, planes + 1] = xhi[h]
    row = lax.broadcasted_iota(jnp.int32, (band, depth), 0)
    column = lax.broadcasted_iota(jnp.int32, (band, depth), 1)
    first_row, last_row = row == 0, row == band - 1
    first_column, last_column = column == 0, column == depth - 1

    def along_y(here, ends):
        down = jnp.where(first_row, ends[0:1], pltpu.roll(here, 1, 0))
        up = jnp.where(last_row, ends[1:2], pltpu.roll(here, band - 1, 0))
        return up - down

    def along_z(here):
        left = jnp.where(first_column, 0.0, pltpu.roll(here, 1, 1))
        right = jnp.where(last_column, 0.0, pltpu.roll(here, depth - 1, 1))
        return right - left

    def step(x, carry):
        px, py, pz = psi[0, x + 1], psi[1, x + 1], psi[2, x + 1]
        velocity[0, x] = 0.5 * (along_y(pz, edge[1, x]) - along_z(py))
        velocity[1, x] = 0.5 * (along_z(px) - (psi[2, x + 2] - psi[2, x]))
        velocity[2, x] = 0.5 * ((psi[1, x + 2] - psi[1, x]) - along_y(px, edge[0, x]))
        return carry

    lax.fori_loop(0, planes, step, 0)


def curl(me, groups, chunks, shape, edges, blocks):
    _, planes, band, depth = shape
    width = planes // groups // chunks
    return pl.pallas_call(
        functools.partial(curl_kernel, groups, chunks, band, width),
        out_shape=jax.ShapeDtypeStruct(shape, jnp.float32),
        in_specs=[pl.BlockSpec(memory_space=SMEM)] + in_vmem(2 + len(blocks)),
        out_specs=pl.BlockSpec(memory_space=VMEM),
        scratch_shapes=[
            pltpu.VMEM((3, planes + 2, band, depth), jnp.float32),
            pltpu.VMEM((2, planes, 2, depth), jnp.float32),
        ],
        compiler_params=params(),
        name="curl",
    )(me, *edges, *blocks)


def pairs(size, step):
    return [(i, i + step) for i in range(size) if 0 <= i + step < size]


def swap(blocks):
    groups = len(blocks)
    moved = [blocks[0]] + [None] * (groups - 1)
    order = sorted(range(1, groups), reverse=True)
    for d in order:
        moved[d] = lax.ppermute(blocks[d], "gy", [(i, i ^ d) for i in range(groups)])
    return moved


def on_device(vorticity, velocity_old, green_hat):
    groups = lax.axis_size("gy")
    across_x = lax.axis_size("gx")
    _, planes, band, depth = vorticity.shape
    rows = band * groups
    per_owner = planes // groups
    chunks = 2 if per_owner % 2 == 0 else 1
    width = per_owner // chunks
    me = lax.axis_index("gy")
    me_array = me.reshape(1)

    fields = (vorticity, velocity_old)
    first_rows = jnp.concatenate([f[:, :, 0] for f in fields], axis=0)
    last_rows = jnp.concatenate([f[:, :, band - 1] for f in fields], axis=0)
    first_x = jnp.concatenate([f[:, 0] for f in fields], axis=0)
    last_x = jnp.concatenate([f[:, planes - 1] for f in fields], axis=0)
    halos = (
        lax.ppermute(last_rows, "gy", pairs(groups, 1)),
        lax.ppermute(first_rows, "gy", pairs(groups, -1)),
        lax.ppermute(last_x, "gx", pairs(across_x, 1)),
        lax.ppermute(first_x, "gx", pairs(across_x, -1)),
    )

    forward_z, inverse_z, ahead, back, dirichlet = constants(rows, depth)
    tables = (jnp.asarray(forward_z), jnp.asarray(inverse_z), jnp.asarray(ahead), jnp.asarray(back))
    gathered = lax.all_gather(green_hat, "gy", axis=1, tiled=True)
    arranged = gathered.reshape(2 * rows // radix, radix, 2 * depth)
    green = jnp.einsum("kj,pqj->kqp", jnp.asarray(dirichlet), arranged, precision=lax.Precision.HIGHEST)
    green = green.reshape(depth, 2 * rows)

    received = []
    vorticity_new = None
    for k in range(chunks):
        whole = k == chunks - 1
        outs = advance(k, chunks, whole, me_array, groups, vorticity, velocity_old, halos)
        if whole:
            vorticity_new, outs = outs[0], outs[1:]
        received.append(swap(list(outs)))
    returned = []
    for k in range(chunks):
        solved = solve(me_array, green, tables, received[k])
        returned.append(swap(list(solved)))

    lines = slice(width * band, 3 * width * band)

    def plane_at(x):
        owner = x // per_owner
        local = x % per_owner
        k = (local // width) ^ (owner & 1) if chunks == 2 else 0
        picked = lax.select_n(lax.bitwise_xor(me, owner), *[
            block[lines].reshape(2, width, band, depth)[:, local % width] for block in returned[k]
        ])
        return picked

    edges = (
        lax.ppermute(plane_at(planes - 1), "gx", pairs(across_x, 1)),
        lax.ppermute(plane_at(0), "gx", pairs(across_x, -1)),
    )
    blocks = [block for group in returned for block in group]
    velocity = curl(me_array, groups, chunks, vorticity.shape, edges, blocks)
    return vorticity_new, velocity


def solution(mesh):
    placed = P(None, "gx", "gy", None)
    return jax.shard_map(
        on_device,
        mesh=mesh,
        in_specs=(placed, placed, P(None, "gy")),
        out_specs=(placed, placed),
        check_vma=False,
    )
```

```python
import functools
import math

import jax
import jax.numpy as jnp
import ml_dtypes
import numpy as np
from jax import lax
from jax.experimental import pallas as pl
from jax.experimental.pallas import tpu as pltpu
from jax.sharding import PartitionSpec as P

time_step = 0.2
viscosity = 0.1
radix = 4
batch = 3
VMEM = pltpu.VMEM
SMEM = pltpu.SMEM


def params(mebibytes):
    return pltpu.CompilerParams(vmem_limit_bytes=mebibytes * 1024 * 1024)


def in_vmem(count):
    return [pl.BlockSpec(memory_space=VMEM)] * count


def halves_np(matrix, axis):


    value = np.asarray(matrix, np.float32)
    high = value.astype(ml_dtypes.bfloat16)
    low = (value - high.astype(np.float32)).astype(ml_dtypes.bfloat16)
    return np.concatenate([high, high, low], axis=axis)


def parts(value, axis):
    high = value.astype(jnp.bfloat16)
    low = (value - high.astype(jnp.float32)).astype(jnp.bfloat16)
    return jnp.concatenate([high, low, high], axis=axis)


@functools.lru_cache(maxsize=None)
def constants(rows, depth):
    long_z, long_y = 2 * depth, 2 * rows
    half = long_y // radix
    k = np.arange(depth)[:, None]
    z = np.arange(depth)[None, :]
    turn = 2.0 * np.pi * (((2 * k + 1) * z) % (2 * long_z)) / (2 * long_z)
    forward_z = halves_np(np.concatenate([np.cos(turn), -np.sin(turn)], axis=0), 1)
    inverse_z = np.concatenate([np.cos(turn), -np.sin(turn)], axis=0) * (2.0 / long_z)
    inverse_z = halves_np(inverse_z.T, 1)
    b = np.arange(half)[:, None]
    p = np.arange(half)[None, :]
    ahead, back = [], []
    for q in range(radix):
        angle = 2.0 * np.pi * ((b * (radix * p + q)) % long_y) / long_y
        c, s = np.cos(angle), np.sin(angle)
        ahead.append(halves_np(np.block([[c, -s], [s, c]]), 0))
        c, s = c.T / long_y, s.T / long_y
        back.append(halves_np(np.block([[c, s], [-s, c]]), 0))
    shift = np.arange(depth)[:, None] + 0.5 - np.arange(long_z)[None, :]
    d = np.arange(1, depth)
    table = 1.0 + 2.0 * np.cos(2.0 * np.pi * np.arange(-2 * long_z, 2 * long_z)[:, None] * d[None, :] / (2 * long_z)).sum(1)
    index = np.rint(2 * shift).astype(np.int64) + 2 * long_z
    return forward_z, inverse_z, np.stack(ahead), np.stack(back), table[index] / long_z


@functools.lru_cache(maxsize=None)
def gain_tables(rows, depth):
    dirichlet = constants(rows, depth)[4]
    long_y, long_z = 2 * rows, 2 * depth
    direct, mirrored, single = [], [], []
    for side in range(2):
        k = side * depth + np.arange(depth)
        direct.append(dirichlet[:, k])
        mirrored.append(dirichlet[:, (long_z - k) % long_z] * (k % depth != 0)[None, :])
        single.append(dirichlet[:, depth - side * depth])
    place = np.arange(long_y)
    lines = radix * (place % (long_y // radix)) + place // (long_y // radix)
    order = np.zeros((2 * long_y, long_y))
    order[lines, place] = 1.0
    order[long_y + (long_y - lines) % long_y, place] = 1.0
    tables = np.stack([np.stack(direct), np.stack(mirrored)], axis=1)
    return tables.astype(np.float32), np.stack(single).astype(np.float32), order.astype(np.float32)


def gain_riders(green_hat, depth):
    near = green_hat.reshape(-1, depth)
    far = green_hat[:, 0].reshape(-1, depth)
    return near, jnp.pad(far, ((0, -far.shape[0] % 8), (0, 0)))


def gains(me, green_hat, near, received, lines):
    groups = len(received)
    half = groups // 2
    long_y, columns = green_hat.shape
    depth = near.shape[1]
    highest = lax.Precision.HIGHEST
    tables, single, order = gain_tables(long_y // 2, depth)
    side, place = me // half, me % half
    blocks = jnp.stack([near] + [received[d][lines:] for d in range(1, half)])
    blocks = jnp.take(blocks, lax.bitwise_xor(place, jnp.arange(half)), axis=0)
    body = blocks.reshape(half, long_y, columns)
    firsts = jnp.stack([received[d][lines : lines + long_y // depth] for d in range(half, groups)])
    column = jnp.take(firsts, place, axis=0).reshape(1, long_y)
    table = jnp.asarray(tables)[side].reshape(2 * depth, half, columns)
    mixed = jnp.einsum("kjc,jmc->km", table, body, precision=highest)
    mixed = mixed.reshape(2, depth, long_y)
    mixed = mixed.at[0].add(jnp.asarray(single)[side][:, None] * column)
    mixed = jnp.concatenate([mixed[0], mixed[1]], axis=1)
    return jnp.dot(mixed, jnp.asarray(order), precision=highest)


def plane_of(owner, local, total):
    return owner * total + jnp.where((owner & 1) == 0, local, total - 1 - local)


def arranged(blocks):
    return [blocks[d] for d in sequence_of(len(blocks))]


def by_step(blocks):
    places = {d: n for n, d in enumerate(sequence_of(len(blocks)))}
    return [blocks[places[d]] for d in range(len(blocks))]


def sequence_of(groups):
    far = list(range(groups - 1, groups // 2 - 1, -1))
    near = list(range(groups // 2 - 1, 0, -1))
    mixed = [0]
    while far or near:
        mixed += far[:1] + near[:1]
        far, near = far[1:], near[1:]
    return mixed


def advance_kernel(groups, chunk, chunks, me_ref, vort, vel, xlo, xhi, ylo, yhi, *rest):
    new, sends = rest[-groups - 5], rest[-groups - 4 : -4]
    frame, block, load_sem, store_sem = rest[-4:]
    _, planes, band, depth = vort.shape
    width = frame.shape[3] - 2
    me = me_ref[0]
    row = lax.broadcasted_iota(jnp.int32, (band, depth), 0)
    column = lax.broadcasted_iota(jnp.int32, (band, depth), 1)
    first_row, last_row = row == 0, row == band - 1
    first_column, last_column = column == 0, column == depth - 1
    sequence = arranged(range(groups))
    place, loads, stores = {}, {}, []
    for d in sequence:
        owner = lax.bitwise_xor(me, d)
        even = (owner & 1) == 0
        low = chunk * width
        start = owner * width * chunks + jnp.where(even, low, width * chunks - width - low)
        base = jnp.clip(start - 1, 0, planes - width - 2)
        place[d] = (even, start, base)
        loads[d] = [
            pltpu.make_async_copy(field.at[:, pl.ds(base, width + 2)], frame.at[d, f], load_sem.at[d, f])
            for f, field in enumerate((vort, vel))
        ]
        for load in loads[d]:
            load.start()
    lines = 3 * width * band
    if chunk == 0:
        near, far = rest[:2]
        for d in sequence[1:]:
            rider = near if d < groups // 2 else far
            target = sends[d].at[pl.ds(lines, rider.shape[0]), :]
            stores.append(pltpu.make_async_copy(rider, target, store_sem.at[d, 1 + width]))
            stores[-1].start()
    for d in sequence:
        even, start, base = place[d]
        for load in loads[d]:
            load.wait()
        for s in range(width):
            x = start + s
            here_at = x - base
            before_at = jnp.maximum(here_at - 1, 0)
            after_at = jnp.minimum(here_at + 1, width + 1)

            def neighbours(f, c):
                slot = 3 * f + c
                here = frame[d, f, c, here_at]
                before, after = frame[d, f, c, before_at], frame[d, f, c, after_at]
                if s == 0:
                    before = jnp.where(x > 0, before, xlo[slot])
                if s == width - 1:
                    after = jnp.where(x < planes - 1, after, xhi[slot])
                down = jnp.where(first_row, ylo[slot, pl.ds(x, 1), :], pltpu.roll(here, 1, 0))
                up = jnp.where(last_row, yhi[slot, pl.ds(x, 1), :], pltpu.roll(here, band - 1, 0))
                left = jnp.where(first_column, 0.0, pltpu.roll(here, 1, 1))
                right = jnp.where(last_column, 0.0, pltpu.roll(here, depth - 1, 1))
                return here, after, before, up, down, right, left

            local = jnp.where(even, s, width - 1 - s)
            w = [frame[d, 0, c, here_at] for c in range(3)]
            for c in range(3):
                _, xp, xm, yp, ym, zp, zm = neighbours(1, c)
                stretch = 0.5 * (w[0] * (xp - xm) + w[1] * (yp - ym) + w[2] * (zp - zm))
                here, xp, xm, yp, ym, zp, zm = neighbours(0, c)
                laplace = xp + xm + yp + ym + zp + zm - 6.0 * here
                line = pl.multiple_of((c * width + local) * band, band)
                block[d, pl.ds(line, band), :] = here + time_step * (stretch + viscosity * laplace)
        stores.append(pltpu.make_async_copy(block.at[d], sends[d].at[pl.ds(0, lines), :], store_sem.at[d, 0]))
        stores[-1].start()
        for s in range(width):
            local = jnp.where(even, s, width - 1 - s)
            for c in range(3):
                line = pl.multiple_of((c * width + local) * band, band)
                source = block.at[d, pl.ds(line, band), :]
                stores.append(pltpu.make_async_copy(source, new.at[c, start + s], store_sem.at[d, 2 + width + 3 * s + c]))
                stores[-1].start()
    for store in stores:
        store.wait()


def advance(chunk, chunks, me, groups, vort, vel, halos, riders, partial):
    _, planes, band, depth = vort.shape
    width = planes // groups // chunks
    lines = 3 * width * band
    more = list(riders) if partial is None else [partial]
    anywhere = pl.BlockSpec(memory_space=pl.ANY)
    shapes = [jax.ShapeDtypeStruct(vort.shape, jnp.float32)]
    for d in range(groups):
        extra = 0 if d == 0 or partial is not None else riders[0 if d < groups // 2 else 1].shape[0]
        shapes.append(jax.ShapeDtypeStruct((lines + extra, depth), jnp.float32))
    out = pl.pallas_call(
        functools.partial(advance_kernel, groups, chunk, chunks),
        out_shape=shapes,
        in_specs=[pl.BlockSpec(memory_space=SMEM)] + [anywhere] * 2 + in_vmem(4)
        + (in_vmem(2) if partial is None else [anywhere]),
        out_specs=[anywhere] * (1 + groups),
        scratch_shapes=[
            pltpu.VMEM((groups, 2, 3, width + 2, band, depth), jnp.float32),
            pltpu.VMEM((groups, lines, depth), jnp.float32),
            pltpu.SemaphoreType.DMA((groups, 2)),
            pltpu.SemaphoreType.DMA((groups, 2 + 4 * width)),
        ],
        input_output_aliases={} if partial is None else {7: 0},
        compiler_params=params(56),
        name=f"advance_{chunk}",
    )(me, vort, vel, *halos, *more)
    return out[0], list(out[1:])


def solve_kernel(groups, stage, width, band, me_ref, fz, bz, ey, by, green, *refs):
    sources, refs = by_step(refs[:groups]), refs[groups:]
    if stage == "second":
        carried, refs = refs[0], refs[1:]
    targets, refs = refs[:groups], refs[groups:]
    if stage == "first":
        carried, refs = refs[0], refs[1:]
    data, psi = refs
    depth = sources[0].shape[1]
    rows = band * groups
    half = rows // 2
    me = me_ref[0]
    pad = 8
    sent = (1, 2) if stage == "first" else (0, 1, 2)
    edged = (2,) if stage == "first" else (0, 2)
    zeros = jnp.zeros((pad, depth), jnp.float32)
    count = 3 * width
    starts = [pl.multiple_of(lax.bitwise_xor(me, d) * band, band) for d in range(groups)]
    for i in range(count):
        psi[i, pl.ds(0, pad), :] = zeros
        psi[i, pl.ds(pad + rows, pad), :] = zeros
        for d in range(groups):
            value = sources[d][pl.ds(i * band, band), :]
            high = value.astype(jnp.bfloat16)
            low = (value - high.astype(jnp.float32)).astype(jnp.bfloat16)
            data[i, pl.ds(starts[d], band), :] = jnp.concatenate([high, low, high], axis=1)

    for begin in range(0, count, batch):
        members = range(begin, begin + batch)
        spectra = [
            lax.dot_general(fz[...], data[i], (((1,), (1,)), ((), ())), preferred_element_type=jnp.float32)
            for i in members
        ]
        total = None
        for q in range(radix):
            lines = []
            for spectrum in spectra:
                low_r, high_r = spectrum[:depth, :half], spectrum[:depth, half:]
                low_i, high_i = spectrum[depth:, :half], spectrum[depth:, half:]
                turned = [
                    lambda: (low_r + high_r, low_i + high_i),
                    lambda: (low_r + high_i, low_i - high_r),
                    lambda: (low_r - high_r, low_i - high_i),
                    lambda: (low_r - high_i, low_i + high_r),
                ][q]()
                lines.append(parts(jnp.concatenate(turned, axis=1), 1))
            freq = jnp.dot(jnp.concatenate(lines, axis=0), ey[q], preferred_element_type=jnp.float32)
            gain = green[:, q * half : (q + 1) * half]
            gain = jnp.concatenate([gain, gain], axis=1)
            lines = [parts(freq[n * depth : (n + 1) * depth] * gain, 1) for n in range(batch)]
            out = jnp.dot(jnp.concatenate(lines, axis=0), by[q], preferred_element_type=jnp.float32)
            re, im = out[:, :half], out[:, half:]
            second = [(re, im), (-im, re), (-re, -im), (im, -re)][q]
            mine = (re, im) + second
            total = mine if total is None else tuple(a + b for a, b in zip(total, mine))
        for n, i in enumerate(members):
            own = [value[n * depth : (n + 1) * depth] for value in total]
            stacked = jnp.concatenate(
                [jnp.concatenate([own[0], own[2]], axis=1), jnp.concatenate([own[1], own[3]], axis=1)], axis=0
            )
            result = jnp.dot(bz[...], parts(stacked, 0), preferred_element_type=jnp.float32)
            psi[i, pl.ds(pad, rows), :] = result.T

    if stage != "plain":
        sign = jnp.where((me & 1) == 0, -1.0, 1.0)
        column = lax.broadcasted_iota(jnp.int32, (rows, depth), 1)
        if stage == "first":
            source = psi.at[0]
            target = 1
        else:
            source = carried.at[width - 1]
            target = 0
        here = sign * source[pl.ds(pad, rows), :]
        up = sign * source[pl.ds(pad + 1, rows), :]
        down = sign * source[pl.ds(pad - 1, rows), :]
        left = jnp.where(column == 0, 0.0, pltpu.roll(here, 1, 1))
        right = jnp.where(column == depth - 1, 0.0, pltpu.roll(here, depth - 1, 1))
        psi[width + target, pl.ds(pad, rows), :] += up - down
        psi[2 * width + target, pl.ds(pad, rows), :] += right - left
        for s in range(width):
            if stage == "first":
                carried[s] = psi[s]
            else:
                psi[s] += carried[s]

    for d in range(groups):
        for a, c in enumerate(sent):
            for s in range(width):
                offset = (a * width + s) * band
                aligned = pl.multiple_of(starts[d] + pad, pad)
                targets[d][pl.ds(offset, band), :] = psi[c * width + s, pl.ds(aligned, band), :]
        for a, c in enumerate(edged):
            for s in range(width):
                offset = len(sent) * width * band + (a * width + s) * 2
                targets[d][pl.ds(offset, 1), :] = psi[c * width + s, pl.ds(starts[d] + pad - 1, 1), :]
                targets[d][pl.ds(offset + 1, 1), :] = psi[c * width + s, pl.ds(starts[d] + pad + band, 1), :]


def solve(stage, width, band, me, green, tables, blocks, carried=()):
    groups = len(blocks)
    depth = blocks[0].shape[1]
    rows = band * groups
    sent, edged = (2, 1) if stage == "first" else (3, 2)
    lines = sent * width * band + 8
    shapes = [jax.ShapeDtypeStruct((lines, depth), jnp.float32)] * groups
    if stage == "first":
        shapes = shapes + [jax.ShapeDtypeStruct((width, rows + 16, depth), jnp.float32)]
    out = pl.pallas_call(
        functools.partial(solve_kernel, groups, stage, width, band),
        out_shape=shapes,
        in_specs=[pl.BlockSpec(memory_space=SMEM)] + in_vmem(5 + groups + len(carried)),
        out_specs=in_vmem(len(shapes)),
        scratch_shapes=[
            pltpu.VMEM((3 * width, rows, 3 * depth), jnp.bfloat16),
            pltpu.VMEM((3 * width, rows + 16, depth), jnp.float32),
        ],
        compiler_params=params(56),
        name="solve_" + stage,
    )(me, *tables, green, *arranged(blocks), *carried)
    return out[:groups], tuple(out[groups:])


def curl_kernel(groups, gauge, width, me_ref, xlo, xhi, *refs):
    chunks = len(refs[:-4]) // groups
    blocks = [block for k in range(chunks) for block in by_step(refs[k * groups : (k + 1) * groups])]
    velocity, front, block, sem = refs[groups * chunks :]
    band, depth = block.shape[3:]
    total = chunks * width
    me = me_ref[0]

    def comps(k):
        return (1, 2) if gauge and k == 0 else (0, 1, 2)

    def read(d, m, c):
        k, s = m // width, m % width
        start = (comps(k).index(c) * width + s) * band
        return blocks[k * groups + d][pl.ds(start, band), :]

    def ends(d, m, c):
        k, s = m // width, m % width
        order = (2,) if len(comps(k)) == 2 else (0, 2)
        start = len(comps(k)) * width * band + (order.index(c) * width + s) * 2
        return blocks[k * groups + d][pl.ds(start, 1), :], blocks[k * groups + d][pl.ds(start + 1, 1), :]

    for h in range(2):
        front[0, h] = xlo[h]
        front[groups + 1, h] = xhi[h]
        for d in range(groups):
            front[lax.bitwise_xor(me, d) + 1, h] = read(d, 0, h + 1)
    row = lax.broadcasted_iota(jnp.int32, (band, depth), 0)
    column = lax.broadcasted_iota(jnp.int32, (band, depth), 1)
    first_row, last_row = row == 0, row == band - 1
    first_column, last_column = column == 0, column == depth - 1

    def along_y(d, m, c):
        here = read(d, m, c)
        below, above = ends(d, m, c)
        down = jnp.where(first_row, below, pltpu.roll(here, 1, 0))
        up = jnp.where(last_row, above, pltpu.roll(here, band - 1, 0))
        return up - down

    def along_z(here):
        left = jnp.where(first_column, 0.0, pltpu.roll(here, 1, 1))
        right = jnp.where(last_column, 0.0, pltpu.roll(here, depth - 1, 1))
        return right - left

    copies = []
    for d in range(groups):
        owner = lax.bitwise_xor(me, d)
        even = (owner & 1) == 0
        sign = jnp.where(even, 0.5, -0.5)
        side = jnp.where(even, owner, owner + 2)

        def along_x(m, c):
            after = read(d, m + 1, c) if m < total - 1 else read(d ^ 1, m, c)
            before = read(d, m - 1, c) if m > 0 else front[side, c - 1]
            return sign * (after - before)

        for m in range(total):
            place = jnp.where(even, m, total - 1 - m)
            no_x = 0 not in comps(m // width)
            block[d, 0, place] = 0.5 * (along_y(d, m, 2) - along_z(read(d, m, 1)))
            first, second = -along_x(m, 2), along_x(m, 1)
            if not no_x:
                first = first + 0.5 * along_z(read(d, m, 0))
                second = second - 0.5 * along_y(d, m, 0)
            block[d, 1, place] = first
            block[d, 2, place] = second
        for c in range(3):
            target = velocity.at[c, pl.ds(owner * total, total)]
            copy = pltpu.make_async_copy(block.at[d, c], target, sem.at[d, c])
            copy.start()
            copies.append(copy)
    for copy in copies:
        copy.wait()


def curl(me, groups, gauge, shape, edges, blocks):
    _, planes, band, depth = shape
    chunks = len(blocks) // groups
    total = planes // groups
    return pl.pallas_call(
        functools.partial(curl_kernel, groups, gauge, total // chunks),
        out_shape=jax.ShapeDtypeStruct(shape, jnp.float32),
        in_specs=[pl.BlockSpec(memory_space=SMEM)] + in_vmem(2 + len(blocks)),
        out_specs=pl.BlockSpec(memory_space=pl.ANY),
        scratch_shapes=[
            pltpu.VMEM((groups + 2, 2, band, depth), jnp.float32),
            pltpu.VMEM((groups, 3, total, band, depth), jnp.float32),
            pltpu.SemaphoreType.DMA((groups, 3)),
        ],
        compiler_params=params(56),
        name="curl",
    )(me, *edges, *blocks)


def outline_kernel(*refs):
    row_low, row_high = refs[:2], refs[2:4]
    first_rows, last_rows = refs[5:]
    _, planes, lines, _ = row_low[0].shape
    for f in range(2):
        for c in range(3):
            for x in range(planes):
                first_rows[3 * f + c, pl.ds(x, 1), :] = row_low[f][c, x, pl.ds(0, 1), :]
                last_rows[3 * f + c, pl.ds(x, 1), :] = row_high[f][c, x, pl.ds(lines - 1, 1), :]


def outline_x_kernel(*refs):
    low, high = refs[:2], refs[2:4]
    first_x, last_x = refs[4:]
    for f in range(2):
        for c in range(3):
            first_x[3 * f + c] = low[f][c, 0]
            last_x[3 * f + c] = high[f][c, 0]


def outline_x(fields):
    _, planes, band, depth = fields[0].shape
    plane = (3, 1, band, depth)
    specs = [pl.BlockSpec(plane, lambda t: (0, 0, 0, 0))] * 2
    specs += [pl.BlockSpec(plane, lambda t: (0, planes - 1, 0, 0))] * 2
    shape = jax.ShapeDtypeStruct((6, band, depth), jnp.float32)
    return pl.pallas_call(
        outline_x_kernel,
        grid=(1,),
        out_shape=[shape] * 2,
        in_specs=specs,
        out_specs=[pl.BlockSpec(shape.shape, lambda t: (0, 0, 0))] * 2,
        compiler_params=params(56),
        name="outline_x",
    )(*fields, *fields)


def outline(fields, after):
    _, planes, band, depth = fields[0].shape
    lines = 8
    row = (3, planes, lines, depth)
    specs = [pl.BlockSpec(row, lambda t: (0, 0, 0, 0))] * 2
    specs += [pl.BlockSpec(row, lambda t: (0, 0, band // lines - 1, 0))] * 2
    specs += [pl.BlockSpec(memory_space=pl.ANY)]
    shape = jax.ShapeDtypeStruct((6, planes, depth), jnp.float32)
    return pl.pallas_call(
        outline_kernel,
        grid=(1,),
        out_shape=[shape] * 2,
        in_specs=specs,
        out_specs=[pl.BlockSpec(shape.shape, lambda t: (0, 0, 0))] * 2,
        compiler_params=params(56),
        name="outline",
    )(*fields, *fields, after)


def pick_kernel(groups, starts, me_ref, *refs):
    blocks, (low, high, sem) = by_step(refs[:groups]), refs[groups:]
    _, band, _ = low.shape
    me = me_ref[0]
    for place, (target, owner) in enumerate(((low, 0), (high, groups - 1))):
        for d in range(groups):

            @pl.when(lax.bitwise_xor(me, owner) == d)
            def _():
                copies = [
                    pltpu.make_async_copy(blocks[d].at[pl.ds(start, band), :], target.at[h], sem.at[place, h])
                    for h, start in enumerate(starts)
                ]
                for copy in copies:
                    copy.start()
                for copy in copies:
                    copy.wait()


def pick(me, starts, band, blocks):
    shape = jax.ShapeDtypeStruct((2, band, blocks[0].shape[1]), jnp.float32)
    return pl.pallas_call(
        functools.partial(pick_kernel, len(blocks), starts),
        out_shape=[shape] * 2,
        in_specs=[pl.BlockSpec(memory_space=SMEM)] + [pl.BlockSpec(memory_space=pl.ANY)] * len(blocks),
        out_specs=in_vmem(2),
        scratch_shapes=[pltpu.SemaphoreType.DMA((2, 2))],
        compiler_params=params(56),
        name="pick",
    )(me, *arranged(blocks))


def pairs(size, step):
    return [(i, i + step) for i in range(size) if 0 <= i + step < size]


def swap(blocks):
    groups = len(blocks)
    moved = [blocks[0]] + [None] * (groups - 1)
    for d in range(1, groups):
        moved[d] = lax.ppermute(blocks[d], "gy", [(i, i ^ d) for i in range(groups)])
    return moved


def on_device(vorticity, velocity_old, green_hat):
    groups = lax.axis_size("gy")
    across_x = lax.axis_size("gx")
    _, planes, band, depth = vorticity.shape
    rows = band * groups
    per_owner = planes // groups
    chunks = 2 if per_owner % 2 == 0 else 1
    width = per_owner // chunks
    me = lax.axis_index("gy")
    me_array = me.reshape(1)

    fields = (vorticity, velocity_old)
    first_x, last_x = outline_x(fields)
    from_x = (
        lax.ppermute(last_x, "gx", pairs(across_x, 1)),
        lax.ppermute(first_x, "gx", pairs(across_x, -1)),
    )
    first_rows, last_rows = outline(fields, first_x)
    halos = from_x + (
        lax.ppermute(last_rows, "gy", pairs(groups, 1)),
        lax.ppermute(first_rows, "gy", pairs(groups, -1)),
    )

    forward_z, inverse_z, ahead, back, _ = constants(rows, depth)
    tables = (jnp.asarray(forward_z), jnp.asarray(inverse_z), jnp.asarray(ahead), jnp.asarray(back))
    received = []
    vorticity_new = None
    riders = gain_riders(green_hat, depth)
    for k in range(chunks):
        vorticity_new, outs = advance(k, chunks, me_array, groups, vorticity, velocity_old, halos, riders, vorticity_new)
        received.append(swap(outs))
        if k == 0:
            green = gains(me, green_hat, riders[0], received[0], 3 * width * band)
    gauge = chunks == 2 and width == 2
    solved, carried = solve("first" if gauge else "plain", width, band, me_array, green, tables, received[0])
    returned = []
    if chunks == 2:
        solved, late = lax.optimization_barrier((solved, arranged(received[1])))
        received[1] = by_step(late)
    returned.append(swap(solved))
    if chunks == 2:
        solved, _ = solve("second" if gauge else "plain", width, band, me_array, green, tables, received[1], carried)
        returned.append(swap(solved))

    base = width * band * (0 if gauge else 1)
    early = returned[0]
    if chunks == 2:
        late = groups // 2 - 1
        early, returned[1][late] = lax.optimization_barrier((arranged(early), returned[1][late]))
        early = by_step(early)
    low, high = pick(me_array, (base, base + width * band), band, early)
    edges = (
        lax.ppermute(high, "gx", pairs(across_x, 1)),
        lax.ppermute(low, "gx", pairs(across_x, -1)),
    )
    blocks = [block for group in returned for block in arranged(group)]
    velocity = curl(me_array, groups, gauge, vorticity.shape, edges, blocks)
    return vorticity_new, velocity


def solution(mesh):
    placed = P(None, "gx", "gy", None)
    return jax.shard_map(
        on_device,
        mesh=mesh,
        in_specs=(placed, placed, P(None, "gy")),
        out_specs=(placed, placed),
        check_vma=False,
    )
```

```python
import functools
import math

import jax
import jax.numpy as jnp
import ml_dtypes
import numpy as np
from jax import lax
from jax.experimental import pallas as pl
from jax.experimental.pallas import tpu as pltpu
from jax.sharding import PartitionSpec as P

time_step = 0.2
viscosity = 0.1
radix = 4
batch = 3
VMEM = pltpu.VMEM
SMEM = pltpu.SMEM


def params(mebibytes):
    return pltpu.CompilerParams(vmem_limit_bytes=mebibytes * 1024 * 1024)


def in_vmem(count):
    return [pl.BlockSpec(memory_space=VMEM)] * count


def halves_np(matrix, axis):


    value = np.asarray(matrix, np.float32)
    high = value.astype(ml_dtypes.bfloat16)
    low = (value - high.astype(np.float32)).astype(ml_dtypes.bfloat16)
    return np.concatenate([high, high, low], axis=axis)


def parts(value, axis):
    high = value.astype(jnp.bfloat16)
    low = (value - high.astype(jnp.float32)).astype(jnp.bfloat16)
    return jnp.concatenate([high, low, high], axis=axis)


@functools.lru_cache(maxsize=None)
def constants(rows, depth):
    long_z, long_y = 2 * depth, 2 * rows
    half = long_y // radix
    k = np.arange(depth)[:, None]
    z = np.arange(depth)[None, :]
    turn = 2.0 * np.pi * (((2 * k + 1) * z) % (2 * long_z)) / (2 * long_z)
    forward_z = halves_np(np.concatenate([np.cos(turn), -np.sin(turn)], axis=0), 1)
    inverse_z = np.concatenate([np.cos(turn), -np.sin(turn)], axis=0) * (2.0 / long_z)
    inverse_z = halves_np(inverse_z.T, 1)
    b = np.arange(half)[:, None]
    p = np.arange(half)[None, :]
    ahead, back = [], []
    for q in range(radix):
        angle = 2.0 * np.pi * ((b * (radix * p + q)) % long_y) / long_y
        c, s = np.cos(angle), np.sin(angle)
        ahead.append(halves_np(np.block([[c, -s], [s, c]]), 0))
        c, s = c.T / long_y, s.T / long_y
        back.append(halves_np(np.block([[c, s], [-s, c]]), 0))
    shift = np.arange(depth)[:, None] + 0.5 - np.arange(long_z)[None, :]
    d = np.arange(1, depth)
    table = 1.0 + 2.0 * np.cos(2.0 * np.pi * np.arange(-2 * long_z, 2 * long_z)[:, None] * d[None, :] / (2 * long_z)).sum(1)
    index = np.rint(2 * shift).astype(np.int64) + 2 * long_z
    return forward_z, inverse_z, np.stack(ahead), np.stack(back), table[index] / long_z


@functools.lru_cache(maxsize=None)
def gain_tables(rows, depth):
    dirichlet = constants(rows, depth)[4]
    long_y, long_z = 2 * rows, 2 * depth
    direct, mirrored, single = [], [], []
    for side in range(2):
        k = side * depth + np.arange(depth)
        direct.append(dirichlet[:, k])
        mirrored.append(dirichlet[:, (long_z - k) % long_z] * (k % depth != 0)[None, :])
        single.append(dirichlet[:, depth - side * depth])
    place = np.arange(long_y)
    lines = radix * (place % (long_y // radix)) + place // (long_y // radix)
    order = np.zeros((2 * long_y, long_y))
    order[lines, place] = 1.0
    order[long_y + (long_y - lines) % long_y, place] = 1.0
    tables = np.stack([np.stack(direct), np.stack(mirrored)], axis=1)
    return tables.astype(np.float32), np.stack(single).astype(np.float32), order.astype(np.float32)


def gain_riders(green_hat, depth):
    near = green_hat.reshape(-1, depth)
    far = green_hat[:, 0].reshape(-1, depth)
    return near, jnp.pad(far, ((0, -far.shape[0] % 8), (0, 0)))


def gains(me, green_hat, near, received, lines):
    groups = len(received)
    half = groups // 2
    long_y, columns = green_hat.shape
    depth = near.shape[1]
    highest = lax.Precision.HIGHEST
    tables, single, order = gain_tables(long_y // 2, depth)
    side, place = me // half, me % half
    blocks = jnp.stack([near] + [received[d][lines:] for d in range(1, half)])
    blocks = jnp.take(blocks, lax.bitwise_xor(place, jnp.arange(half)), axis=0)
    body = blocks.reshape(half, long_y, columns)
    firsts = jnp.stack([received[d][lines : lines + long_y // depth] for d in range(half, groups)])
    column = jnp.take(firsts, place, axis=0).reshape(1, long_y)
    table = jnp.asarray(tables)[side].reshape(2 * depth, half, columns)
    mixed = jnp.einsum("kjc,jmc->km", table, body, precision=highest)
    mixed = mixed.reshape(2, depth, long_y)
    mixed = mixed.at[0].add(jnp.asarray(single)[side][:, None] * column)
    mixed = jnp.concatenate([mixed[0], mixed[1]], axis=1)
    return jnp.dot(mixed, jnp.asarray(order), precision=highest)


def plane_of(owner, local, total):
    return owner * total + jnp.where((owner & 1) == 0, local, total - 1 - local)


def arranged(blocks, back=False):
    return [blocks[d] for d in sequence_of(len(blocks), back)]


def by_step(blocks, back=False):
    places = {d: n for n, d in enumerate(sequence_of(len(blocks), back))}
    return [blocks[places[d]] for d in range(len(blocks))]


def sequence_of(groups, back):
    if back:
        return [0] + list(range(groups - 1, 0, -1))
    far = list(range(groups - 1, groups // 2 - 1, -1))
    near = list(range(groups // 2 - 1, 0, -1))
    mixed = [0]
    while far or near:
        mixed += far[:1] + near[:1]
        far, near = far[1:], near[1:]
    return mixed


def advance_kernel(steps, chunk, chunks, me_ref, vort, vel, xlo, xhi, ylo, yhi, *rest):
    new, sends = rest[-len(steps) - 5], rest[-len(steps) - 4 : -4]
    frame, block, load_sem, store_sem = rest[-4:]
    _, planes, band, depth = vort.shape
    width = frame.shape[3] - 2
    me = me_ref[0]
    row = lax.broadcasted_iota(jnp.int32, (band, depth), 0)
    column = lax.broadcasted_iota(jnp.int32, (band, depth), 1)
    first_row, last_row = row == 0, row == band - 1
    first_column, last_column = column == 0, column == depth - 1
    place, loads, stores = {}, {}, []
    for n, d in enumerate(steps):
        owner = lax.bitwise_xor(me, d)
        even = (owner & 1) == 0
        low = chunk * width
        start = owner * width * chunks + jnp.where(even, low, width * chunks - width - low)
        base = jnp.clip(start - 1, 0, planes - width - 2)
        place[n] = (even, start, base)
        loads[n] = [
            pltpu.make_async_copy(field.at[:, pl.ds(base, width + 2)], frame.at[n, f], load_sem.at[n, f])
            for f, field in enumerate((vort, vel))
        ]
        for load in loads[n]:
            load.start()
    lines = 3 * width * band
    if sends[-1].shape[0] > lines:
        rider = rest[0]
        for n, d in enumerate(steps):
            if d > 0:
                target = sends[n].at[pl.ds(lines, rider.shape[0]), :]
                stores.append(pltpu.make_async_copy(rider, target, store_sem.at[n, 1 + width]))
                stores[-1].start()
    for n in range(len(steps)):
        even, start, base = place[n]
        for load in loads[n]:
            load.wait()
        for s in range(width):
            x = start + s
            here_at = x - base
            before_at = jnp.maximum(here_at - 1, 0)
            after_at = jnp.minimum(here_at + 1, width + 1)

            def neighbours(f, c):
                slot = 3 * f + c
                here = frame[n, f, c, here_at]
                before, after = frame[n, f, c, before_at], frame[n, f, c, after_at]
                if s == 0:
                    before = jnp.where(x > 0, before, xlo[slot])
                if s == width - 1:
                    after = jnp.where(x < planes - 1, after, xhi[slot])
                down = jnp.where(first_row, ylo[slot, pl.ds(x, 1), :], pltpu.roll(here, 1, 0))
                up = jnp.where(last_row, yhi[slot, pl.ds(x, 1), :], pltpu.roll(here, band - 1, 0))
                left = jnp.where(first_column, 0.0, pltpu.roll(here, 1, 1))
                right = jnp.where(last_column, 0.0, pltpu.roll(here, depth - 1, 1))
                return here, after, before, up, down, right, left

            local = jnp.where(even, s, width - 1 - s)
            w = [frame[n, 0, c, here_at] for c in range(3)]
            for c in range(3):
                _, xp, xm, yp, ym, zp, zm = neighbours(1, c)
                stretch = 0.5 * (w[0] * (xp - xm) + w[1] * (yp - ym) + w[2] * (zp - zm))
                here, xp, xm, yp, ym, zp, zm = neighbours(0, c)
                laplace = xp + xm + yp + ym + zp + zm - 6.0 * here
                line = pl.multiple_of((c * width + local) * band, band)
                block[n, pl.ds(line, band), :] = here + time_step * (stretch + viscosity * laplace)
        stores.append(pltpu.make_async_copy(block.at[n], sends[n].at[pl.ds(0, lines), :], store_sem.at[n, 0]))
        stores[-1].start()
        for s in range(width):
            local = jnp.where(even, s, width - 1 - s)
            for c in range(3):
                line = pl.multiple_of((c * width + local) * band, band)
                source = block.at[n, pl.ds(line, band), :]
                stores.append(pltpu.make_async_copy(source, new.at[c, start + s], store_sem.at[n, 2 + width + 3 * s + c]))
                stores[-1].start()
    for store in stores:
        store.wait()


def advance(steps, chunk, chunks, me, groups, vort, vel, halos, rider, partial):
    _, planes, band, depth = vort.shape
    width = planes // groups // chunks
    lines = 3 * width * band
    anywhere = pl.BlockSpec(memory_space=pl.ANY)
    more = [v for v in (rider, partial) if v is not None]
    specs = ([] if rider is None else in_vmem(1)) + ([] if partial is None else [anywhere])
    shapes = [jax.ShapeDtypeStruct(vort.shape, jnp.float32)]
    for d in steps:
        extra = 0 if d == 0 or rider is None else rider.shape[0]
        shapes.append(jax.ShapeDtypeStruct((lines + extra, depth), jnp.float32))
    out = pl.pallas_call(
        functools.partial(advance_kernel, steps, chunk, chunks),
        out_shape=shapes,
        in_specs=[pl.BlockSpec(memory_space=SMEM)] + [anywhere] * 2 + in_vmem(4) + specs,
        out_specs=[anywhere] * (1 + len(steps)),
        scratch_shapes=[
            pltpu.VMEM((len(steps), 2, 3, width + 2, band, depth), jnp.float32),
            pltpu.VMEM((len(steps), lines, depth), jnp.float32),
            pltpu.SemaphoreType.DMA((len(steps), 2)),
            pltpu.SemaphoreType.DMA((len(steps), 2 + 4 * width)),
        ],
        input_output_aliases={} if partial is None else {6 + len(more): 0},
        compiler_params=params(56),
        name=f"advance_{chunk}_{len(more)}",
    )(me, vort, vel, *halos, *more)
    return out[0], list(out[1:])


def solve_kernel(groups, stage, width, band, me_ref, fz, bz, ey, by, green, *refs):
    sources, refs = by_step(refs[:groups]), refs[groups:]
    if stage == "second":
        carried, refs = refs[0], refs[1:]
    targets, refs = refs[:groups], refs[groups:]
    if stage == "first":
        carried, refs = refs[0], refs[1:]
    data, psi = refs
    depth = sources[0].shape[1]
    rows = band * groups
    half = rows // 2
    me = me_ref[0]
    pad = 8
    sent = (1, 2) if stage == "first" else (0, 1, 2)
    edged = (2,) if stage == "first" else (0, 2)
    zeros = jnp.zeros((pad, depth), jnp.float32)
    count = 3 * width
    starts = [pl.multiple_of(lax.bitwise_xor(me, d) * band, band) for d in range(groups)]
    for i in range(count):
        psi[i, pl.ds(0, pad), :] = zeros
        psi[i, pl.ds(pad + rows, pad), :] = zeros
        for d in range(groups):
            value = sources[d][pl.ds(i * band, band), :]
            high = value.astype(jnp.bfloat16)
            low = (value - high.astype(jnp.float32)).astype(jnp.bfloat16)
            data[i, pl.ds(starts[d], band), :] = jnp.concatenate([high, low, high], axis=1)

    for begin in range(0, count, batch):
        members = range(begin, begin + batch)
        spectra = [
            lax.dot_general(fz[...], data[i], (((1,), (1,)), ((), ())), preferred_element_type=jnp.float32)
            for i in members
        ]
        total = None
        for q in range(radix):
            lines = []
            for spectrum in spectra:
                low_r, high_r = spectrum[:depth, :half], spectrum[:depth, half:]
                low_i, high_i = spectrum[depth:, :half], spectrum[depth:, half:]
                turned = [
                    lambda: (low_r + high_r, low_i + high_i),
                    lambda: (low_r + high_i, low_i - high_r),
                    lambda: (low_r - high_r, low_i - high_i),
                    lambda: (low_r - high_i, low_i + high_r),
                ][q]()
                lines.append(parts(jnp.concatenate(turned, axis=1), 1))
            freq = jnp.dot(jnp.concatenate(lines, axis=0), ey[q], preferred_element_type=jnp.float32)
            gain = green[:, q * half : (q + 1) * half]
            gain = jnp.concatenate([gain, gain], axis=1)
            lines = [parts(freq[n * depth : (n + 1) * depth] * gain, 1) for n in range(batch)]
            out = jnp.dot(jnp.concatenate(lines, axis=0), by[q], preferred_element_type=jnp.float32)
            re, im = out[:, :half], out[:, half:]
            second = [(re, im), (-im, re), (-re, -im), (im, -re)][q]
            mine = (re, im) + second
            total = mine if total is None else tuple(a + b for a, b in zip(total, mine))
        for n, i in enumerate(members):
            own = [value[n * depth : (n + 1) * depth] for value in total]
            stacked = jnp.concatenate(
                [jnp.concatenate([own[0], own[2]], axis=1), jnp.concatenate([own[1], own[3]], axis=1)], axis=0
            )
            result = jnp.dot(bz[...], parts(stacked, 0), preferred_element_type=jnp.float32)
            psi[i, pl.ds(pad, rows), :] = result.T

    if stage != "plain":
        sign = jnp.where((me & 1) == 0, -1.0, 1.0)
        column = lax.broadcasted_iota(jnp.int32, (rows, depth), 1)
        if stage == "first":
            source = psi.at[0]
            target = 1
        else:
            source = carried.at[width - 1]
            target = 0
        here = sign * source[pl.ds(pad, rows), :]
        up = sign * source[pl.ds(pad + 1, rows), :]
        down = sign * source[pl.ds(pad - 1, rows), :]
        left = jnp.where(column == 0, 0.0, pltpu.roll(here, 1, 1))
        right = jnp.where(column == depth - 1, 0.0, pltpu.roll(here, depth - 1, 1))
        psi[width + target, pl.ds(pad, rows), :] += up - down
        psi[2 * width + target, pl.ds(pad, rows), :] += right - left
        for s in range(width):
            if stage == "first":
                carried[s] = psi[s]
            else:
                psi[s] += carried[s]

    for d in range(groups):
        for a, c in enumerate(sent):
            for s in range(width):
                offset = (a * width + s) * band
                aligned = pl.multiple_of(starts[d] + pad, pad)
                targets[d][pl.ds(offset, band), :] = psi[c * width + s, pl.ds(aligned, band), :]
        for a, c in enumerate(edged):
            for s in range(width):
                offset = len(sent) * width * band + (a * width + s) * 2
                targets[d][pl.ds(offset, 1), :] = psi[c * width + s, pl.ds(starts[d] + pad - 1, 1), :]
                targets[d][pl.ds(offset + 1, 1), :] = psi[c * width + s, pl.ds(starts[d] + pad + band, 1), :]


def solve(stage, width, band, me, green, tables, blocks, carried=()):
    groups = len(blocks)
    depth = blocks[0].shape[1]
    rows = band * groups
    sent, edged = (2, 1) if stage == "first" else (3, 2)
    lines = sent * width * band + 8
    shapes = [jax.ShapeDtypeStruct((lines, depth), jnp.float32)] * groups
    if stage == "first":
        shapes = shapes + [jax.ShapeDtypeStruct((width, rows + 16, depth), jnp.float32)]
    out = pl.pallas_call(
        functools.partial(solve_kernel, groups, stage, width, band),
        out_shape=shapes,
        in_specs=[pl.BlockSpec(memory_space=SMEM)] + in_vmem(5 + groups + len(carried)),
        out_specs=in_vmem(len(shapes)),
        scratch_shapes=[
            pltpu.VMEM((3 * width, rows, 3 * depth), jnp.bfloat16),
            pltpu.VMEM((3 * width, rows + 16, depth), jnp.float32),
        ],
        compiler_params=params(56),
        name="solve_" + stage,
    )(me, *tables, green, *arranged(blocks), *carried)
    return out[:groups], tuple(out[groups:])


def curl_kernel(groups, gauge, width, me_ref, xlo, xhi, *refs):
    chunks = len(refs[:-4]) // groups
    blocks = [block for k in range(chunks) for block in by_step(refs[k * groups : (k + 1) * groups], True)]
    velocity, front, block, sem = refs[groups * chunks :]
    band, depth = block.shape[3:]
    total = chunks * width
    me = me_ref[0]

    def comps(k):
        return (1, 2) if gauge and k == 0 else (0, 1, 2)

    def read(d, m, c):
        k, s = m // width, m % width
        start = (comps(k).index(c) * width + s) * band
        return blocks[k * groups + d][pl.ds(start, band), :]

    def ends(d, m, c):
        k, s = m // width, m % width
        order = (2,) if len(comps(k)) == 2 else (0, 2)
        start = len(comps(k)) * width * band + (order.index(c) * width + s) * 2
        return blocks[k * groups + d][pl.ds(start, 1), :], blocks[k * groups + d][pl.ds(start + 1, 1), :]

    for h in range(2):
        front[0, h] = xlo[h]
        front[groups + 1, h] = xhi[h]
        for d in range(groups):
            front[lax.bitwise_xor(me, d) + 1, h] = read(d, 0, h + 1)
    row = lax.broadcasted_iota(jnp.int32, (band, depth), 0)
    column = lax.broadcasted_iota(jnp.int32, (band, depth), 1)
    first_row, last_row = row == 0, row == band - 1
    first_column, last_column = column == 0, column == depth - 1

    def along_y(d, m, c):
        here = read(d, m, c)
        below, above = ends(d, m, c)
        down = jnp.where(first_row, below, pltpu.roll(here, 1, 0))
        up = jnp.where(last_row, above, pltpu.roll(here, band - 1, 0))
        return up - down

    def along_z(here):
        left = jnp.where(first_column, 0.0, pltpu.roll(here, 1, 1))
        right = jnp.where(last_column, 0.0, pltpu.roll(here, depth - 1, 1))
        return right - left

    copies = []
    for d in range(groups):
        owner = lax.bitwise_xor(me, d)
        even = (owner & 1) == 0
        sign = jnp.where(even, 0.5, -0.5)
        side = jnp.where(even, owner, owner + 2)

        def along_x(m, c):
            after = read(d, m + 1, c) if m < total - 1 else read(d ^ 1, m, c)
            before = read(d, m - 1, c) if m > 0 else front[side, c - 1]
            return sign * (after - before)

        for m in range(total):
            place = jnp.where(even, m, total - 1 - m)
            no_x = 0 not in comps(m // width)
            block[d, 0, place] = 0.5 * (along_y(d, m, 2) - along_z(read(d, m, 1)))
            first, second = -along_x(m, 2), along_x(m, 1)
            if not no_x:
                first = first + 0.5 * along_z(read(d, m, 0))
                second = second - 0.5 * along_y(d, m, 0)
            block[d, 1, place] = first
            block[d, 2, place] = second
        for c in range(3):
            target = velocity.at[c, pl.ds(owner * total, total)]
            copy = pltpu.make_async_copy(block.at[d, c], target, sem.at[d, c])
            copy.start()
            copies.append(copy)
    for copy in copies:
        copy.wait()


def curl(me, groups, gauge, shape, edges, blocks):
    _, planes, band, depth = shape
    chunks = len(blocks) // groups
    total = planes // groups
    return pl.pallas_call(
        functools.partial(curl_kernel, groups, gauge, total // chunks),
        out_shape=jax.ShapeDtypeStruct(shape, jnp.float32),
        in_specs=[pl.BlockSpec(memory_space=SMEM)] + in_vmem(2 + len(blocks)),
        out_specs=pl.BlockSpec(memory_space=pl.ANY),
        scratch_shapes=[
            pltpu.VMEM((groups + 2, 2, band, depth), jnp.float32),
            pltpu.VMEM((groups, 3, total, band, depth), jnp.float32),
            pltpu.SemaphoreType.DMA((groups, 3)),
        ],
        compiler_params=params(56),
        name="curl",
    )(me, *edges, *blocks)


def outline_kernel(*refs):
    row_low, row_high, x_low, x_high = refs[:2], refs[2:4], refs[4:6], refs[6:8]
    first_rows, last_rows, first_x, last_x = refs[8:]
    _, planes, lines, _ = row_low[0].shape
    for f in range(2):
        for c in range(3):
            first_x[3 * f + c] = x_low[f][c, 0]
            last_x[3 * f + c] = x_high[f][c, 0]
            for x in range(planes):
                first_rows[3 * f + c, pl.ds(x, 1), :] = row_low[f][c, x, pl.ds(0, 1), :]
                last_rows[3 * f + c, pl.ds(x, 1), :] = row_high[f][c, x, pl.ds(lines - 1, 1), :]


def outline(fields):
    _, planes, band, depth = fields[0].shape
    lines = 8
    row = (3, planes, lines, depth)
    plane = (3, 1, band, depth)
    specs = [pl.BlockSpec(row, lambda t: (0, 0, 0, 0))] * 2
    specs += [pl.BlockSpec(row, lambda t: (0, 0, band // lines - 1, 0))] * 2
    specs += [pl.BlockSpec(plane, lambda t: (0, 0, 0, 0))] * 2
    specs += [pl.BlockSpec(plane, lambda t: (0, planes - 1, 0, 0))] * 2
    shapes = [jax.ShapeDtypeStruct((6, planes, depth), jnp.float32)] * 2
    shapes += [jax.ShapeDtypeStruct((6, band, depth), jnp.float32)] * 2
    return pl.pallas_call(
        outline_kernel,
        grid=(1,),
        out_shape=shapes,
        in_specs=specs,
        out_specs=[pl.BlockSpec(v.shape, lambda t: (0, 0, 0)) for v in shapes],
        compiler_params=params(56),
        name="outline",
    )(*fields, *fields, *fields, *fields)


def pick_kernel(groups, starts, me_ref, *refs):
    blocks, (low, high, sem) = by_step(refs[:groups], True), refs[groups:]
    _, band, _ = low.shape
    me = me_ref[0]
    for place, (target, owner) in enumerate(((low, 0), (high, groups - 1))):
        for d in range(groups):

            @pl.when(lax.bitwise_xor(me, owner) == d)
            def _():
                copies = [
                    pltpu.make_async_copy(blocks[d].at[pl.ds(start, band), :], target.at[h], sem.at[place, h])
                    for h, start in enumerate(starts)
                ]
                for copy in copies:
                    copy.start()
                for copy in copies:
                    copy.wait()


def pick(me, starts, band, blocks):
    shape = jax.ShapeDtypeStruct((2, band, blocks[0].shape[1]), jnp.float32)
    return pl.pallas_call(
        functools.partial(pick_kernel, len(blocks), starts),
        out_shape=[shape] * 2,
        in_specs=[pl.BlockSpec(memory_space=SMEM)] + [pl.BlockSpec(memory_space=pl.ANY)] * len(blocks),
        out_specs=in_vmem(2),
        scratch_shapes=[pltpu.SemaphoreType.DMA((2, 2))],
        compiler_params=params(56),
        name="pick",
    )(me, *arranged(blocks, True))


def pairs(size, step):
    return [(i, i + step) for i in range(size) if 0 <= i + step < size]


def swap(blocks):
    groups = len(blocks)
    moved = [blocks[0]] + [None] * (groups - 1)
    for d in range(1, groups):
        moved[d] = lax.ppermute(blocks[d], "gy", [(i, i ^ d) for i in range(groups)])
    return moved


def on_device(vorticity, velocity_old, green_hat):
    groups = lax.axis_size("gy")
    across_x = lax.axis_size("gx")
    _, planes, band, depth = vorticity.shape
    rows = band * groups
    per_owner = planes // groups
    chunks = 2 if per_owner % 2 == 0 else 1
    width = per_owner // chunks
    me = lax.axis_index("gy")
    me_array = me.reshape(1)

    fields = (vorticity, velocity_old)
    first_rows, last_rows, first_x, last_x = outline(fields)
    from_x = (
        lax.ppermute(last_x, "gx", pairs(across_x, 1)),
        lax.ppermute(first_x, "gx", pairs(across_x, -1)),
    )
    halos = from_x + (
        lax.ppermute(last_rows, "gy", pairs(groups, 1)),
        lax.ppermute(first_rows, "gy", pairs(groups, -1)),
    )

    forward_z, inverse_z, ahead, back, _ = constants(rows, depth)
    tables = (jnp.asarray(forward_z), jnp.asarray(inverse_z), jnp.asarray(ahead), jnp.asarray(back))
    received = []
    vorticity_new = None
    riders = gain_riders(green_hat, depth)
    for k in range(chunks):
        fixed = (me_array, groups, vorticity, velocity_old, halos)
        if k == 0:
            far, near = tuple(range(groups - 1, groups // 2 - 1, -1)), tuple(range(groups // 2))
            vorticity_new, late = advance(far, k, chunks, *fixed, riders[1], None)
            vorticity_new, outs = advance(near, k, chunks, *fixed, riders[0], vorticity_new)
            outs = outs + late[::-1]
        else:
            vorticity_new, outs = advance(tuple(range(groups)), k, chunks, *fixed, None, vorticity_new)
        received.append(swap(outs))
        if k == 0:
            green = gains(me, green_hat, riders[0], received[0], 3 * width * band)
    gauge = chunks == 2 and width == 2
    solved, carried = solve("first" if gauge else "plain", width, band, me_array, green, tables, received[0])
    returned = []
    if chunks == 2:
        solved, late = lax.optimization_barrier((solved, arranged(received[1])))
        received[1] = by_step(late)
    returned.append(swap(solved))
    if chunks == 2:
        solved, _ = solve("second" if gauge else "plain", width, band, me_array, green, tables, received[1], carried)
        returned.append(swap(solved))

    base = width * band * (0 if gauge else 1)
    early = returned[0]
    if chunks == 2:
        late = groups // 2 - 1
        early, returned[1][late] = lax.optimization_barrier((arranged(early, True), returned[1][late]))
        early = by_step(early, True)
    low, high = pick(me_array, (base, base + width * band), band, early)
    edges = (
        lax.ppermute(high, "gx", pairs(across_x, 1)),
        lax.ppermute(low, "gx", pairs(across_x, -1)),
    )
    blocks = [block for group in returned for block in arranged(group, True)]
    velocity = curl(me_array, groups, gauge, vorticity.shape, edges, blocks)
    return vorticity_new, velocity


def solution(mesh):
    placed = P(None, "gx", "gy", None)
    return jax.shard_map(
        on_device,
        mesh=mesh,
        in_specs=(placed, placed, P(None, "gy")),
        out_specs=(placed, placed),
        check_vma=False,
    )
```

```python
import functools
import math

import jax
import jax.numpy as jnp
import ml_dtypes
import numpy as np
from jax import lax
from jax.experimental import pallas as pl
from jax.experimental.pallas import tpu as pltpu
from jax.sharding import PartitionSpec as P

time_step = 0.2
viscosity = 0.1
radix = 4
batch = 3
VMEM = pltpu.VMEM
SMEM = pltpu.SMEM


def params(mebibytes):
    return pltpu.CompilerParams(vmem_limit_bytes=mebibytes * 1024 * 1024)


def in_vmem(count):
    return [pl.BlockSpec(memory_space=VMEM)] * count


def halves_np(matrix, axis):


    value = np.asarray(matrix, np.float32)
    high = value.astype(ml_dtypes.bfloat16)
    low = (value - high.astype(np.float32)).astype(ml_dtypes.bfloat16)
    return np.concatenate([high, high, low], axis=axis)


def parts(value, axis):
    high = value.astype(jnp.bfloat16)
    low = (value - high.astype(jnp.float32)).astype(jnp.bfloat16)
    return jnp.concatenate([high, low, high], axis=axis)


@functools.lru_cache(maxsize=None)
def constants(rows, depth):
    long_z, long_y = 2 * depth, 2 * rows
    half = long_y // radix
    k = np.arange(depth)[:, None]
    z = np.arange(depth)[None, :]
    turn = 2.0 * np.pi * (((2 * k + 1) * z) % (2 * long_z)) / (2 * long_z)
    forward_z = halves_np(np.concatenate([np.cos(turn), -np.sin(turn)], axis=0), 1)
    inverse_z = np.concatenate([np.cos(turn), -np.sin(turn)], axis=0) * (2.0 / long_z)
    inverse_z = halves_np(inverse_z.T, 1)
    b = np.arange(half)[:, None]
    p = np.arange(half)[None, :]
    ahead, back = [], []
    for q in range(radix):
        angle = 2.0 * np.pi * ((b * (radix * p + q)) % long_y) / long_y
        c, s = np.cos(angle), np.sin(angle)
        ahead.append(halves_np(np.block([[c, -s], [s, c]]), 0))
        c, s = c.T / long_y, s.T / long_y
        back.append(halves_np(np.block([[c, s], [-s, c]]), 0))
    shift = np.arange(depth)[:, None] + 0.5 - np.arange(long_z)[None, :]
    d = np.arange(1, depth)
    table = 1.0 + 2.0 * np.cos(2.0 * np.pi * np.arange(-2 * long_z, 2 * long_z)[:, None] * d[None, :] / (2 * long_z)).sum(1)
    index = np.rint(2 * shift).astype(np.int64) + 2 * long_z
    return forward_z, inverse_z, np.stack(ahead), np.stack(back), table[index] / long_z


@functools.lru_cache(maxsize=None)
def gain_tables(rows, depth):
    dirichlet = constants(rows, depth)[4]
    long_y, long_z = 2 * rows, 2 * depth
    direct, mirrored, single = [], [], []
    for side in range(2):
        k = side * depth + np.arange(depth)
        direct.append(dirichlet[:, k])
        mirrored.append(dirichlet[:, (long_z - k) % long_z] * (k % depth != 0)[None, :])
        single.append(dirichlet[:, depth - side * depth])
    place = np.arange(long_y)
    lines = radix * (place % (long_y // radix)) + place // (long_y // radix)
    order = np.zeros((2 * long_y, long_y))
    order[lines, place] = 1.0
    order[long_y + (long_y - lines) % long_y, place] = 1.0
    tables = np.stack([np.stack(direct), np.stack(mirrored)], axis=1)
    return tables.astype(np.float32), np.stack(single).astype(np.float32), order.astype(np.float32)


def gain_riders(green_hat, depth):
    near = green_hat.reshape(-1, depth)
    far = green_hat[:, 0].reshape(-1, depth)
    return near, jnp.pad(far, ((0, -far.shape[0] % 8), (0, 0)))


def gains(me, green_hat, near, received, lines):
    groups = len(received)
    half = groups // 2
    long_y, columns = green_hat.shape
    depth = near.shape[1]
    highest = lax.Precision.HIGHEST
    tables, single, order = gain_tables(long_y // 2, depth)
    side, place = me // half, me % half
    blocks = jnp.stack([near] + [received[d][lines:] for d in range(1, half)])
    blocks = jnp.take(blocks, lax.bitwise_xor(place, jnp.arange(half)), axis=0)
    body = blocks.reshape(half, long_y, columns)
    firsts = jnp.stack([received[d][lines : lines + long_y // depth] for d in range(half, groups)])
    column = jnp.take(firsts, place, axis=0).reshape(1, long_y)
    table = jnp.asarray(tables)[side].reshape(2 * depth, half, columns)
    mixed = jnp.einsum("kjc,jmc->km", table, body, precision=highest)
    mixed = mixed.reshape(2, depth, long_y)
    mixed = mixed.at[0].add(jnp.asarray(single)[side][:, None] * column)
    mixed = jnp.concatenate([mixed[0], mixed[1]], axis=1)
    return jnp.dot(mixed, jnp.asarray(order), precision=highest)


def plane_of(owner, local, total):
    return owner * total + jnp.where((owner & 1) == 0, local, total - 1 - local)


def arranged(blocks, back=False):
    return [blocks[d] for d in sequence_of(len(blocks), back)]


def by_step(blocks, back=False):
    places = {d: n for n, d in enumerate(sequence_of(len(blocks), back))}
    return [blocks[places[d]] for d in range(len(blocks))]


def sequence_of(groups, back):
    if back:
        return [0] + list(range(groups - 1, 0, -1))
    far = list(range(groups - 1, groups // 2 - 1, -1))
    near = list(range(groups // 2 - 1, 0, -1))
    mixed = [0]
    while far or near:
        mixed += far[:1] + near[:1]
        far, near = far[1:], near[1:]
    return mixed


def advance_kernel(steps, chunk, chunks, me_ref, vort, vel, xlo, xhi, ylo, yhi, *rest):
    new, sends = rest[-len(steps) - 5], rest[-len(steps) - 4 : -4]
    frame, block, load_sem, store_sem = rest[-4:]
    _, planes, band, depth = vort.shape
    width = frame.shape[3] - 2
    me = me_ref[0]
    row = lax.broadcasted_iota(jnp.int32, (band, depth), 0)
    column = lax.broadcasted_iota(jnp.int32, (band, depth), 1)
    first_row, last_row = row == 0, row == band - 1
    first_column, last_column = column == 0, column == depth - 1
    place, loads, stores = {}, {}, []
    for n, d in enumerate(steps):
        owner = lax.bitwise_xor(me, d)
        even = (owner & 1) == 0
        low = chunk * width
        start = owner * width * chunks + jnp.where(even, low, width * chunks - width - low)
        base = jnp.clip(start - 1, 0, planes - width - 2)
        place[n] = (even, start, base)
        loads[n] = [
            pltpu.make_async_copy(field.at[:, pl.ds(base, width + 2)], frame.at[n, f], load_sem.at[n, f])
            for f, field in enumerate((vort, vel))
        ]
        for load in loads[n]:
            load.start()
    lines = 3 * width * band
    if sends[-1].shape[0] > lines:
        rider = rest[0]
        for n, d in enumerate(steps):
            if d > 0:
                target = sends[n].at[pl.ds(lines, rider.shape[0]), :]
                stores.append(pltpu.make_async_copy(rider, target, store_sem.at[n, 1 + width]))
                stores[-1].start()
    for n in range(len(steps)):
        even, start, base = place[n]
        for load in loads[n]:
            load.wait()
        for s in range(width):
            x = start + s
            here_at = x - base
            before_at = jnp.maximum(here_at - 1, 0)
            after_at = jnp.minimum(here_at + 1, width + 1)

            def neighbours(f, c):
                slot = 3 * f + c
                here = frame[n, f, c, here_at]
                before, after = frame[n, f, c, before_at], frame[n, f, c, after_at]
                if s == 0:
                    before = jnp.where(x > 0, before, xlo[slot])
                if s == width - 1:
                    after = jnp.where(x < planes - 1, after, xhi[slot])
                down = jnp.where(first_row, ylo[slot, pl.ds(x, 1), :], pltpu.roll(here, 1, 0))
                up = jnp.where(last_row, yhi[slot, pl.ds(x, 1), :], pltpu.roll(here, band - 1, 0))
                left = jnp.where(first_column, 0.0, pltpu.roll(here, 1, 1))
                right = jnp.where(last_column, 0.0, pltpu.roll(here, depth - 1, 1))
                return here, after, before, up, down, right, left

            local = jnp.where(even, s, width - 1 - s)
            w = [frame[n, 0, c, here_at] for c in range(3)]
            for c in range(3):
                _, xp, xm, yp, ym, zp, zm = neighbours(1, c)
                stretch = 0.5 * (w[0] * (xp - xm) + w[1] * (yp - ym) + w[2] * (zp - zm))
                here, xp, xm, yp, ym, zp, zm = neighbours(0, c)
                laplace = xp + xm + yp + ym + zp + zm - 6.0 * here
                line = pl.multiple_of((c * width + local) * band, band)
                block[n, pl.ds(line, band), :] = here + time_step * (stretch + viscosity * laplace)
        stores.append(pltpu.make_async_copy(block.at[n], sends[n].at[pl.ds(0, lines), :], store_sem.at[n, 0]))
        stores[-1].start()
        for s in range(width):
            local = jnp.where(even, s, width - 1 - s)
            for c in range(3):
                line = pl.multiple_of((c * width + local) * band, band)
                source = block.at[n, pl.ds(line, band), :]
                stores.append(pltpu.make_async_copy(source, new.at[c, start + s], store_sem.at[n, 2 + width + 3 * s + c]))
                stores[-1].start()
    for store in stores:
        store.wait()


def advance(steps, chunk, chunks, me, groups, vort, vel, halos, rider, partial):
    _, planes, band, depth = vort.shape
    width = planes // groups // chunks
    lines = 3 * width * band
    anywhere = pl.BlockSpec(memory_space=pl.ANY)
    more = [v for v in (rider, partial) if v is not None]
    specs = ([] if rider is None else in_vmem(1)) + ([] if partial is None else [anywhere])
    shapes = [jax.ShapeDtypeStruct(vort.shape, jnp.float32)]
    for d in steps:
        extra = 0 if d == 0 or rider is None else rider.shape[0]
        shapes.append(jax.ShapeDtypeStruct((lines + extra, depth), jnp.float32))
    out = pl.pallas_call(
        functools.partial(advance_kernel, steps, chunk, chunks),
        out_shape=shapes,
        in_specs=[pl.BlockSpec(memory_space=SMEM)] + [anywhere] * 2 + in_vmem(4) + specs,
        out_specs=[anywhere] * (1 + len(steps)),
        scratch_shapes=[
            pltpu.VMEM((len(steps), 2, 3, width + 2, band, depth), jnp.float32),
            pltpu.VMEM((len(steps), lines, depth), jnp.float32),
            pltpu.SemaphoreType.DMA((len(steps), 2)),
            pltpu.SemaphoreType.DMA((len(steps), 2 + 4 * width)),
        ],
        input_output_aliases={} if partial is None else {6 + len(more): 0},
        compiler_params=params(56),
        name=f"advance_{chunk}_{len(more)}",
    )(me, vort, vel, *halos, *more)
    return out[0], list(out[1:])


def solve_kernel(groups, stage, width, band, me_ref, fz, bz, ey, by, green, *refs):
    sources, refs = by_step(refs[:groups]), refs[groups:]
    if stage == "second":
        carried, refs = refs[0], refs[1:]
    targets, refs = refs[:groups], refs[groups:]
    if stage == "first":
        carried, refs = refs[0], refs[1:]
    data, psi = refs
    depth = sources[0].shape[1]
    rows = band * groups
    half = rows // 2
    me = me_ref[0]
    pad = 8
    sent = (1, 2) if stage == "first" else (0, 1, 2)
    edged = (2,) if stage == "first" else (0, 2)
    zeros = jnp.zeros((pad, depth), jnp.float32)
    count = 3 * width
    starts = [pl.multiple_of(lax.bitwise_xor(me, d) * band, band) for d in range(groups)]
    for i in range(count):
        psi[i, pl.ds(0, pad), :] = zeros
        psi[i, pl.ds(pad + rows, pad), :] = zeros
        for d in range(groups):
            value = sources[d][pl.ds(i * band, band), :]
            high = value.astype(jnp.bfloat16)
            low = (value - high.astype(jnp.float32)).astype(jnp.bfloat16)
            data[i, pl.ds(starts[d], band), :] = jnp.concatenate([high, low, high], axis=1)

    for begin in range(0, count, batch):
        members = range(begin, begin + batch)
        spectra = [
            lax.dot_general(fz[...], data[i], (((1,), (1,)), ((), ())), preferred_element_type=jnp.float32)
            for i in members
        ]
        total = None
        for q in range(radix):
            lines = []
            for spectrum in spectra:
                low_r, high_r = spectrum[:depth, :half], spectrum[:depth, half:]
                low_i, high_i = spectrum[depth:, :half], spectrum[depth:, half:]
                turned = [
                    lambda: (low_r + high_r, low_i + high_i),
                    lambda: (low_r + high_i, low_i - high_r),
                    lambda: (low_r - high_r, low_i - high_i),
                    lambda: (low_r - high_i, low_i + high_r),
                ][q]()
                lines.append(parts(jnp.concatenate(turned, axis=1), 1))
            freq = jnp.dot(jnp.concatenate(lines, axis=0), ey[q], preferred_element_type=jnp.float32)
            gain = green[:, q * half : (q + 1) * half]
            gain = jnp.concatenate([gain, gain], axis=1)
            lines = [parts(freq[n * depth : (n + 1) * depth] * gain, 1) for n in range(batch)]
            out = jnp.dot(jnp.concatenate(lines, axis=0), by[q], preferred_element_type=jnp.float32)
            re, im = out[:, :half], out[:, half:]
            second = [(re, im), (-im, re), (-re, -im), (im, -re)][q]
            mine = (re, im) + second
            total = mine if total is None else tuple(a + b for a, b in zip(total, mine))
        for n, i in enumerate(members):
            own = [value[n * depth : (n + 1) * depth] for value in total]
            stacked = jnp.concatenate(
                [jnp.concatenate([own[0], own[2]], axis=1), jnp.concatenate([own[1], own[3]], axis=1)], axis=0
            )
            result = jnp.dot(bz[...], parts(stacked, 0), preferred_element_type=jnp.float32)
            psi[i, pl.ds(pad, rows), :] = result.T

    if stage != "plain":
        sign = jnp.where((me & 1) == 0, -1.0, 1.0)
        column = lax.broadcasted_iota(jnp.int32, (rows, depth), 1)
        if stage == "first":
            source = psi.at[0]
            target = 1
        else:
            source = carried.at[width - 1]
            target = 0
        here = sign * source[pl.ds(pad, rows), :]
        up = sign * source[pl.ds(pad + 1, rows), :]
        down = sign * source[pl.ds(pad - 1, rows), :]
        left = jnp.where(column == 0, 0.0, pltpu.roll(here, 1, 1))
        right = jnp.where(column == depth - 1, 0.0, pltpu.roll(here, depth - 1, 1))
        psi[width + target, pl.ds(pad, rows), :] += up - down
        psi[2 * width + target, pl.ds(pad, rows), :] += right - left
        for s in range(width):
            if stage == "first":
                carried[s] = psi[s]
            else:
                psi[s] += carried[s]

    for d in range(groups):
        for a, c in enumerate(sent):
            for s in range(width):
                offset = (a * width + s) * band
                aligned = pl.multiple_of(starts[d] + pad, pad)
                targets[d][pl.ds(offset, band), :] = psi[c * width + s, pl.ds(aligned, band), :]
        for a, c in enumerate(edged):
            for s in range(width):
                offset = len(sent) * width * band + (a * width + s) * 2
                targets[d][pl.ds(offset, 1), :] = psi[c * width + s, pl.ds(starts[d] + pad - 1, 1), :]
                targets[d][pl.ds(offset + 1, 1), :] = psi[c * width + s, pl.ds(starts[d] + pad + band, 1), :]


def solve(stage, width, band, me, green, tables, blocks, carried=()):
    groups = len(blocks)
    depth = blocks[0].shape[1]
    rows = band * groups
    sent, edged = (2, 1) if stage == "first" else (3, 2)
    lines = sent * width * band + 8
    shapes = [jax.ShapeDtypeStruct((lines, depth), jnp.float32)] * groups
    if stage == "first":
        shapes = shapes + [jax.ShapeDtypeStruct((width, rows + 16, depth), jnp.float32)]
    out = pl.pallas_call(
        functools.partial(solve_kernel, groups, stage, width, band),
        out_shape=shapes,
        in_specs=[pl.BlockSpec(memory_space=SMEM)] + in_vmem(5 + groups + len(carried)),
        out_specs=in_vmem(len(shapes)),
        scratch_shapes=[
            pltpu.VMEM((3 * width, rows, 3 * depth), jnp.bfloat16),
            pltpu.VMEM((3 * width, rows + 16, depth), jnp.float32),
        ],
        compiler_params=params(56),
        name="solve_" + stage,
    )(me, *tables, green, *arranged(blocks), *carried)
    return out[:groups], tuple(out[groups:])


def curl_kernel(groups, gauge, width, me_ref, xlo, xhi, *refs):
    chunks = len(refs[:-4]) // groups
    blocks = [block for k in range(chunks) for block in by_step(refs[k * groups : (k + 1) * groups], True)]
    velocity, front, block, sem = refs[groups * chunks :]
    band, depth = block.shape[3:]
    total = chunks * width
    me = me_ref[0]

    def comps(k):
        return (1, 2) if gauge and k == 0 else (0, 1, 2)

    def read(d, m, c):
        k, s = m // width, m % width
        start = (comps(k).index(c) * width + s) * band
        return blocks[k * groups + d][pl.ds(start, band), :]

    def ends(d, m, c):
        k, s = m // width, m % width
        order = (2,) if len(comps(k)) == 2 else (0, 2)
        start = len(comps(k)) * width * band + (order.index(c) * width + s) * 2
        return blocks[k * groups + d][pl.ds(start, 1), :], blocks[k * groups + d][pl.ds(start + 1, 1), :]

    for h in range(2):
        front[0, h] = xlo[h]
        front[groups + 1, h] = xhi[h]
        for d in range(groups):
            front[lax.bitwise_xor(me, d) + 1, h] = read(d, 0, h + 1)
    row = lax.broadcasted_iota(jnp.int32, (band, depth), 0)
    column = lax.broadcasted_iota(jnp.int32, (band, depth), 1)
    first_row, last_row = row == 0, row == band - 1
    first_column, last_column = column == 0, column == depth - 1

    def along_y(d, m, c):
        here = read(d, m, c)
        below, above = ends(d, m, c)
        down = jnp.where(first_row, below, pltpu.roll(here, 1, 0))
        up = jnp.where(last_row, above, pltpu.roll(here, band - 1, 0))
        return up - down

    def along_z(here):
        left = jnp.where(first_column, 0.0, pltpu.roll(here, 1, 1))
        right = jnp.where(last_column, 0.0, pltpu.roll(here, depth - 1, 1))
        return right - left

    copies = []
    for d in range(groups):
        owner = lax.bitwise_xor(me, d)
        even = (owner & 1) == 0
        sign = jnp.where(even, 0.5, -0.5)
        side = jnp.where(even, owner, owner + 2)

        def along_x(m, c):
            after = read(d, m + 1, c) if m < total - 1 else read(d ^ 1, m, c)
            before = read(d, m - 1, c) if m > 0 else front[side, c - 1]
            return sign * (after - before)

        for m in range(total):
            place = jnp.where(even, m, total - 1 - m)
            no_x = 0 not in comps(m // width)
            block[d, 0, place] = 0.5 * (along_y(d, m, 2) - along_z(read(d, m, 1)))
            first, second = -along_x(m, 2), along_x(m, 1)
            if not no_x:
                first = first + 0.5 * along_z(read(d, m, 0))
                second = second - 0.5 * along_y(d, m, 0)
            block[d, 1, place] = first
            block[d, 2, place] = second
        for c in range(3):
            target = velocity.at[c, pl.ds(owner * total, total)]
            copy = pltpu.make_async_copy(block.at[d, c], target, sem.at[d, c])
            copy.start()
            copies.append(copy)
    for copy in copies:
        copy.wait()


def curl(me, groups, gauge, shape, edges, blocks):
    _, planes, band, depth = shape
    chunks = len(blocks) // groups
    total = planes // groups
    return pl.pallas_call(
        functools.partial(curl_kernel, groups, gauge, total // chunks),
        out_shape=jax.ShapeDtypeStruct(shape, jnp.float32),
        in_specs=[pl.BlockSpec(memory_space=SMEM)] + in_vmem(2 + len(blocks)),
        out_specs=pl.BlockSpec(memory_space=pl.ANY),
        scratch_shapes=[
            pltpu.VMEM((groups + 2, 2, band, depth), jnp.float32),
            pltpu.VMEM((groups, 3, total, band, depth), jnp.float32),
            pltpu.SemaphoreType.DMA((groups, 3)),
        ],
        compiler_params=params(56),
        name="curl",
    )(me, *edges, *blocks)


def outline_kernel(*refs):
    row_low, row_high, x_low, x_high = refs[:2], refs[2:4], refs[4:6], refs[6:8]
    first_rows, last_rows, first_x, last_x = refs[8:]
    _, planes, lines, _ = row_low[0].shape
    for f in range(2):
        for c in range(3):
            first_x[3 * f + c] = x_low[f][c, 0]
            last_x[3 * f + c] = x_high[f][c, 0]
            for x in range(planes):
                first_rows[3 * f + c, pl.ds(x, 1), :] = row_low[f][c, x, pl.ds(0, 1), :]
                last_rows[3 * f + c, pl.ds(x, 1), :] = row_high[f][c, x, pl.ds(lines - 1, 1), :]


def outline(fields):
    _, planes, band, depth = fields[0].shape
    lines = 8
    row = (3, planes, lines, depth)
    plane = (3, 1, band, depth)
    specs = [pl.BlockSpec(row, lambda t: (0, 0, 0, 0))] * 2
    specs += [pl.BlockSpec(row, lambda t: (0, 0, band // lines - 1, 0))] * 2
    specs += [pl.BlockSpec(plane, lambda t: (0, 0, 0, 0))] * 2
    specs += [pl.BlockSpec(plane, lambda t: (0, planes - 1, 0, 0))] * 2
    shapes = [jax.ShapeDtypeStruct((6, planes, depth), jnp.float32)] * 2
    shapes += [jax.ShapeDtypeStruct((6, band, depth), jnp.float32)] * 2
    return pl.pallas_call(
        outline_kernel,
        grid=(1,),
        out_shape=shapes,
        in_specs=specs,
        out_specs=[pl.BlockSpec(v.shape, lambda t: (0, 0, 0)) for v in shapes],
        compiler_params=params(56),
        name="outline",
    )(*fields, *fields, *fields, *fields)


def pick_kernel(groups, starts, me_ref, *refs):
    blocks, (low, high, sem) = by_step(refs[:groups], True), refs[groups:]
    _, band, _ = low.shape
    me = me_ref[0]
    for place, (target, owner) in enumerate(((low, 0), (high, groups - 1))):
        for d in range(groups):

            @pl.when(lax.bitwise_xor(me, owner) == d)
            def _():
                copies = [
                    pltpu.make_async_copy(blocks[d].at[pl.ds(start, band), :], target.at[h], sem.at[place, h])
                    for h, start in enumerate(starts)
                ]
                for copy in copies:
                    copy.start()
                for copy in copies:
                    copy.wait()


def pick(me, starts, band, blocks):
    shape = jax.ShapeDtypeStruct((2, band, blocks[0].shape[1]), jnp.float32)
    return pl.pallas_call(
        functools.partial(pick_kernel, len(blocks), starts),
        out_shape=[shape] * 2,
        in_specs=[pl.BlockSpec(memory_space=SMEM)] + [pl.BlockSpec(memory_space=pl.ANY)] * len(blocks),
        out_specs=in_vmem(2),
        scratch_shapes=[pltpu.SemaphoreType.DMA((2, 2))],
        compiler_params=params(56),
        name="pick",
    )(me, *arranged(blocks, True))


def pairs(size, step):
    return [(i, i + step) for i in range(size) if 0 <= i + step < size]


def swap(blocks):
    groups = len(blocks)
    moved = [blocks[0]] + [None] * (groups - 1)
    for d in range(1, groups):
        moved[d] = lax.ppermute(blocks[d], "gy", [(i, i ^ d) for i in range(groups)])
    return moved


def on_device(vorticity, velocity_old, green_hat):
    groups = lax.axis_size("gy")
    across_x = lax.axis_size("gx")
    _, planes, band, depth = vorticity.shape
    rows = band * groups
    per_owner = planes // groups
    chunks = 2 if per_owner % 2 == 0 else 1
    width = per_owner // chunks
    me = lax.axis_index("gy")
    me_array = me.reshape(1)

    fields = (vorticity, velocity_old)
    first_rows, last_rows, first_x, last_x = outline(fields)
    from_x = (
        lax.ppermute(last_x, "gx", pairs(across_x, 1)),
        lax.ppermute(first_x, "gx", pairs(across_x, -1)),
    )
    halos = from_x + (
        lax.ppermute(last_rows, "gy", pairs(groups, 1)),
        lax.ppermute(first_rows, "gy", pairs(groups, -1)),
    )

    forward_z, inverse_z, ahead, back, _ = constants(rows, depth)
    tables = (jnp.asarray(forward_z), jnp.asarray(inverse_z), jnp.asarray(ahead), jnp.asarray(back))
    received = []
    vorticity_new = None
    riders = gain_riders(green_hat, depth)
    for k in range(chunks):
        fixed = (me_array, groups, vorticity, velocity_old, halos)
        if k == 0:
            far, near = tuple(range(groups - 1, groups // 2 - 1, -1)), tuple(range(groups // 2))
            vorticity_new, late = advance(far, k, chunks, *fixed, riders[1], None)
            vorticity_new, outs = advance(near, k, chunks, *fixed, riders[0], vorticity_new)
            outs = outs + late[::-1]
        else:
            vorticity_new, outs = advance(tuple(range(groups)), k, chunks, *fixed, None, vorticity_new)
        received.append(swap(outs))
        if k == 0:
            green = gains(me, green_hat, riders[0], received[0], 3 * width * band)
    gauge = chunks == 2 and width == 2
    solved, carried = solve("first" if gauge else "plain", width, band, me_array, green, tables, received[0])
    returned = []
    if chunks == 2:
        solved, late = lax.optimization_barrier((solved, arranged(received[1])))
        received[1] = by_step(late)
    returned.append(swap(solved))
    if chunks == 2:
        solved, _ = solve("second" if gauge else "plain", width, band, me_array, green, tables, received[1], carried)
        returned.append(swap(solved))

    base = width * band * (0 if gauge else 1)
    early = returned[0]
    if chunks == 2:
        late = 1
        early, returned[1][late] = lax.optimization_barrier((arranged(early, True), returned[1][late]))
        early = by_step(early, True)
    low, high = pick(me_array, (base, base + width * band), band, early)
    edges = (
        lax.ppermute(high, "gx", pairs(across_x, 1)),
        lax.ppermute(low, "gx", pairs(across_x, -1)),
    )
    blocks = [block for group in returned for block in arranged(group, True)]
    velocity = curl(me_array, groups, gauge, vorticity.shape, edges, blocks)
    return vorticity_new, velocity


def solution(mesh):
    placed = P(None, "gx", "gy", None)
    return jax.shard_map(
        on_device,
        mesh=mesh,
        in_specs=(placed, placed, P(None, "gy")),
        out_specs=(placed, placed),
        check_vma=False,
    )
```
